256 devices in a mesh: rep: 2 (over z_hi), section: 16 (over y, x), tp: 8 (over z_lo, core).
Axes of the slice: x: 4, y: 4, z: 8 (z_hi: 2, z_lo: 4; z = z_hi * 4 + z_lo), core: 2. Of those that a mesh axis runs over, the one named last changes fastest.
Arguments:
- upstream: bfloat16 [2, 16, 352, 8192], P('rep', 'section', None, 'tp'), may hold values from -720 to 720
- norm_gain: float32 [8192], P('tp'), may hold values from 0.25 to 1.75
- grad_values: bfloat16 [2, 16, 352, 1024], P('rep', 'section'), may hold values from -6 to 6
- grad_other: bfloat16 [2, 16, 352, 8192], P('rep', 'section', None, 'tp'), may hold values from -8 to 8
- local_weights: bfloat16 [2, 16, 8192, 1024], P('rep', 'section', 'tp'), may hold values from -6 to 6
- anchor: bfloat16 [2, 16, 8192, 1024], P('rep', 'section', 'tp'), may hold values from -6 to 6
- momentum: bfloat16 [2, 16, 8192, 1024], P('rep', 'section', 'tp'), may hold values from -3 to 3
- section_routes: int32 [16, 2], replicated, may hold values from 0 to 1, as said below
- pairing: int32 [16, 2], replicated, may hold values from 0 to 1, each once within a row
Outputs:
- values: bfloat16 [2, 16, 352, 1024], P('rep', 'section', 'tp')
- input_grad_returned: bfloat16 [2, 16, 352, 8192], P('rep', 'section', None, 'tp')
- anchor_new: bfloat16 [2, 16, 8192, 1024], P('rep', 'section', 'tp')
- momentum_new: bfloat16 [2, 16, 8192, 1024], P('rep', 'section', 'tp')
The draws below stay inside these ranges and needn't reach their ends.
Inputs may be any that keep to these rules, and one draw needn't show every extreme that they name: `section_routes`: each row is a permutation of the replicas 0 to 1. Each row is a pairing: pairing[s, pairing[s, r]] = r; a replica paired with itself keeps its own outer gradient.
All inputs are finite; a program needn't handle non-finite values.
Results may differ from the reference program's by a relative error of at most 0.0054.
Values may be sent and summed in bfloat16 or wider, within the bound.
A program may use at most 64 MiB of HBM per device.

```python
import math
import jax
import jax.numpy as jnp
from jax import lax

D = 8192
VW = 1024
TOK = 352
N_REP = 2
N_SECTION = 16
N_TP = 8


def shared_bits(key):
    return jax.random.randint(jax.random.fold_in(key, 101), (N_SECTION,), 0, 2)


def shared_normal(key):
    return jax.random.truncated_normal(jax.random.fold_in(key, 102), -4.0, 4.0, (N_REP, N_SECTION, TOK, D), jnp.float32)


def draw_section_routes(key, part):
    flip_bits = shared_bits(key)
    return jnp.stack([flip_bits, 1 - flip_bits], axis=1).astype(jnp.int32)


def draw_upstream(key, part):
    normals = shared_normal(key)
    key = jax.random.fold_in(key, 1)
    key_rows, key_cols, key_blocks = jax.random.split(key, 3)
    column_ids = jnp.arange(D)
    block_ids = column_ids * N_TP // D
    rising = 1.0 + 2.0 * block_ids.astype(jnp.float32) / max(N_TP - 1, 1)
    columns = jnp.exp(jax.random.uniform(key_cols, (D,), jnp.float32, 0.0, math.log(10.0)))
    blocks = jnp.exp(jax.random.uniform(key_blocks, (N_REP, N_SECTION, TOK, N_TP), jnp.float32, 0.0, math.log(2.0)))
    spread_blocks = blocks[..., block_ids]
    row_scales = jnp.exp(jax.random.uniform(key_rows, (N_REP, N_SECTION, TOK, 1), jnp.float32, math.log(0.3), math.log(3.0)))
    base_values = normals
    return (base_values * row_scales * columns * rising * spread_blocks).astype(jnp.bfloat16)


def draw_grad_other(key, part):
    normals = shared_normal(key)
    flip_bits = shared_bits(key)
    key = jax.random.fold_in(key, 2)
    earlier = jnp.roll(normals, 1, axis=1)
    crossed = earlier[::-1]
    pick_cross = jnp.roll(flip_bits, 1)[None, :, None, None]
    aligned = jnp.where(pick_cross == 1, crossed, earlier)
    noise_part = jax.random.truncated_normal(key, -4.0, 4.0, (N_REP, N_SECTION, TOK, D), jnp.float32)
    return (aligned + noise_part).astype(jnp.bfloat16)


def steps_of(stream_key, dims, cuts, smallest, largest):
    def one(dim, parts):
        heights = jax.random.uniform(jax.random.fold_in(jax.random.fold_in(stream_key, 6), dim), (parts,), jnp.float32, smallest / len(cuts), largest / len(cuts))
        return jnp.repeat(jnp.exp(heights), dims[dim] // parts).reshape((-1,) + (1,) * (len(dims) - dim - 1))

    gain = one(*cuts[0])
    for cut in cuts[1:]:
        gain = gain * one(*cut)
    return gain


def scatter_about(key, extent, width, limit, cuts=(), kind=jnp.bfloat16):
    result = width * jax.random.normal(key, extent, jnp.float32)
    if cuts:
        result = result * steps_of(key, extent, cuts, -0.22, 0.18)
    return jnp.clip(result, -limit, limit).astype(kind)


def setup_inputs(seed: int = 0) -> dict:
    arg_keys = jax.random.split(jax.random.key(seed), 10)
    return {
        "upstream": draw_upstream(jax.random.fold_in(arg_keys[9], 71), 0),
        "norm_gain": jnp.clip(1.0 + 0.15 * jax.random.normal(arg_keys[1], (D,), jnp.float32), 0.25, 1.75),
        "grad_values": scatter_about(arg_keys[2], (N_REP, N_SECTION, TOK, VW), 1.0, 6.0, ((0, 2), (1, 16))),
        "grad_other": draw_grad_other(jax.random.fold_in(arg_keys[9], 71), 0),
        "local_weights": scatter_about(arg_keys[4], (N_REP, N_SECTION, D, VW), 1.0, 6.0, ((0, 2), (1, 16), (2, 8))),
        "anchor": scatter_about(arg_keys[5], (N_REP, N_SECTION, D, VW), 1.0, 6.0, ((0, 2), (1, 16), (2, 8))),
        "momentum": scatter_about(arg_keys[6], (N_REP, N_SECTION, D, VW), 0.5, 3.0, ((0, 2), (1, 16), (2, 8))),
        "section_routes": draw_section_routes(jax.random.fold_in(arg_keys[9], 71), 0),
        "pairing": jax.vmap(lambda own: jax.random.permutation(own, N_REP))(jax.random.split(arg_keys[8], N_SECTION)).reshape((N_SECTION, N_REP)).astype(jnp.int32),
    }


eps = 1e-05
inner_rate = 1.0
outer_rate = 0.7
keep_rate = 0.9

def to_section_major(array):
    return jnp.swapaxes(array, 0, 1)

def reference(upstream, norm_gain, grad_values, grad_other, local_weights, anchor, momentum, section_routes, pairing):
    scale = D ** (-0.5)
    section_ids = jnp.arange(N_SECTION, dtype=jnp.int32)
    replica_ids = jnp.arange(N_REP, dtype=jnp.int32)
    earlier_routes = jnp.roll(section_routes, 1, axis=0)
    source = lax.optimization_barrier(jnp.sum(jnp.where(earlier_routes[:, :, None] == replica_ids[None, None, :], replica_ids[None, :, None], 0), axis=1)).astype(jnp.int32)
    earlier_states = jnp.roll(upstream, 1, axis=1)
    arrived = earlier_states[source.T, section_ids[None, :]]

    def one_replica(tokens_in, grad_vals, grad_more, weights):
        floated = tokens_in.astype(jnp.float32)
        inv_rms = lax.rsqrt(lax.optimization_barrier(jnp.mean(floated * floated, axis=-1, keepdims=True)) + eps)
        normed = (floated * inv_rms * norm_gain).astype(jnp.bfloat16)
        values = (jnp.dot(normed, weights, preferred_element_type=jnp.float32) * scale).astype(jnp.bfloat16)
        grad_normed = jnp.dot(grad_vals, weights.T, preferred_element_type=jnp.float32) * scale + grad_more.astype(jnp.float32)
        row_dot = lax.optimization_barrier(jnp.sum(floated * norm_gain * grad_normed, axis=-1, keepdims=True))
        grad_input = (inv_rms * norm_gain * grad_normed - floated * inv_rms ** 3 * row_dot / D).astype(jnp.bfloat16)
        weight_grad = jnp.dot(normed.T, grad_vals, preferred_element_type=jnp.float32) * scale
        return (values, grad_input, weight_grad)

    def one_section(section_item):
        tokens_in, grad_vals, grad_more, weights, anchor_block, momentum_block, pair_row = section_item
        values, grad_input, weight_grad = jax.vmap(one_replica)(tokens_in, grad_vals, grad_more, weights)
        local_new = weights.astype(jnp.float32) - inner_rate * weight_grad
        outer_grad = (anchor_block.astype(jnp.float32) - local_new).astype(jnp.bfloat16)
        partner_grad = outer_grad[pair_row]
        mean_grad = 0.5 * (outer_grad.astype(jnp.float32) + partner_grad.astype(jnp.float32))
        momentum_next = keep_rate * momentum_block.astype(jnp.float32) + mean_grad
        anchor_new = (anchor_block.astype(jnp.float32) - outer_rate * (mean_grad + keep_rate * momentum_next)).astype(jnp.bfloat16)
        return (values, grad_input, anchor_new, momentum_next.astype(jnp.bfloat16))
    values, grad_input, anchor_new, momentum_new = lax.map(one_section, (to_section_major(arrived), to_section_major(grad_values), to_section_major(grad_other), to_section_major(local_weights), to_section_major(anchor), to_section_major(momentum), pairing))
    values = to_section_major(values)
    grad_input = to_section_major(grad_input)
    anchor_new = to_section_major(anchor_new)
    momentum_new = to_section_major(momentum_new)
    later_grads = jnp.roll(grad_input, -1, axis=1)
    returned = later_grads[section_routes.T, section_ids[None, :]]
    return (values, returned, anchor_new, momentum_new)
```

```python
import functools

import jax
import jax.numpy as jnp
from jax import lax
from jax.experimental import pallas as pl
from jax.experimental.pallas import tpu as pltpu
from jax.sharding import PartitionSpec as P

MESH = pl.DeviceIdType.MESH
F32 = jnp.float32
BF16 = jnp.bfloat16

D = 8192
eps = 1e-05
inner_rate = 1.0
outer_rate = 0.7
keep_rate = 0.9
scale = D ** (-0.5)

TOK = 352
PAD = 384
OWN = 44
ROWS = 48
W = 1024
LANE = 128
BLOCKS = W // LANE


def remote(src, dst, send_sem, recv_sem, device):
    return pltpu.make_async_remote_copy(
        src_ref=src, dst_ref=dst, send_sem=send_sem, recv_sem=recv_sem,
        device_id=device, device_id_type=MESH,
    )


def lanes(j):
    return pl.ds(pl.multiple_of(j * LANE, LANE), LANE)


def kernel(
    up_hbm, gain_ref, gv_hbm, go_hbm, w_hbm, a_hbm, m_hbm, in_mask, back_mask, pair_mask,
    val_out, ret_out, anc_out, mom_out,
    near, far, gv, go, w, a, m, gn, normed, padded, parts, stat_send, stat_recv,
    inv_ref, dot_ref, grad, back_near, back_far, og, og_recv, anc, mom, vals, vsend, vrecv, zsend, zrecv, vout,
    load_sem, fwd_send, fwd_recv, back_send, back_recv, stat_ss, stat_rs, og_ss, og_rs, core_sem, z_ss, z_rs, out_sem,
):
    rep = lax.axis_index("rep")
    sec = lax.axis_index("section")
    tp = lax.axis_index("tp")
    core = lax.rem(tp, 2)
    zlo = tp // 2
    other = 1 - rep
    after = lax.rem(sec + 1, 16)
    before = lax.rem(sec + 15, 16)
    sibling = 2 * zlo + 1 - core

    loads = [
        pltpu.make_async_copy(src, dst, load_sem.at[i])
        for i, (src, dst) in enumerate(
            [(gv_hbm, gv), (w_hbm, w), (go_hbm, go), (a_hbm, a), (m_hbm, m)]
        )
    ]
    for load in loads:
        load.start()

    barrier = pltpu.get_barrier_semaphore()
    peers = [(rep, after, tp), (other, after, tp), (rep, before, tp), (other, before, tp), (other, sec, tp)]
    peers += [(rep, sec, lax.rem(tp + d, 8)) for d in range(1, 8)]
    for peer in peers:
        pl.semaphore_signal(barrier, inc=1, device_id=peer, device_id_type=MESH)
    pl.semaphore_wait(barrier, len(peers))

    fwd = [
        remote(up_hbm, far, fwd_send.at[0], fwd_recv.at[0], (other, after, tp)),
        remote(up_hbm, near, fwd_send.at[1], fwd_recv.at[1], (rep, after, tp)),
    ]
    for copy in fwd:
        copy.start()

    for load in loads[:3]:
        load.wait()

    def grad_normed(j, _):
        cols = lanes(j)
        product = lax.dot_general(
            gv[...], w[cols, :], (((1,), (1,)), ((), ())), preferred_element_type=F32
        )
        gn[:, cols] = product * scale + go[:, cols].astype(F32)
        return _

    lax.fori_loop(0, BLOCKS, grad_normed, 0)
    parts[...] = jnp.zeros_like(parts)

    for copy in fwd:
        copy.wait()

    take_near = in_mask[...] != 0

    def statistics(j, _):
        cols = lanes(j)
        x = jnp.where(take_near, near[:, cols].astype(F32), far[:, cols].astype(F32))
        near[:, cols] = x.astype(BF16)
        parts[0, 0:TOK, :] += x * x
        parts[1, 0:TOK, :] += x * gain_ref[:, cols] * gn[:, cols]
        return _

    lax.fori_loop(0, BLOCKS, statistics, 0)

    ones = jnp.full((8, LANE), 1.0, F32)
    for i in range(2):
        row = lax.dot_general(
            ones, parts[i], (((1,), (1,)), ((), ())),
            preferred_element_type=F32, precision=lax.Precision.HIGHEST,
        )
        stat_send[i] = row
        stat_recv[i, 0] = row
    stat_copies = []
    for d in range(1, 8):
        copy = remote(
            stat_send, stat_recv.at[:, d], stat_ss.at[d], stat_rs.at[d],
            (rep, sec, lax.rem(tp + d, 8)),
        )
        copy.start()
        stat_copies.append(copy)
    for copy in stat_copies:
        copy.wait()

    eighth = jnp.full((64, LANE), 0.125, F32)
    sums = [
        lax.dot_general(
            stat_recv[i].reshape(64, PAD), eighth, (((0,), (0,)), ((), ())),
            preferred_element_type=F32, precision=lax.Precision.HIGHEST,
        )
        for i in range(2)
    ]
    inv = lax.rsqrt(sums[0][0:TOK] / D + eps)
    inv_ref[...] = inv
    dot_ref[...] = inv * inv * inv * sums[1][0:TOK] / D

    def input_gradient(j, _):
        cols = lanes(j)
        x = near[:, cols].astype(F32)
        gain = gain_ref[:, cols]
        inv = inv_ref[...]
        grad[:, cols] = (inv * gain * gn[:, cols] - x * dot_ref[...]).astype(BF16)
        normed[:, cols] = (x * inv * gain).astype(BF16)
        return _

    lax.fori_loop(0, BLOCKS, input_gradient, 0)
    back = [
        remote(grad, back_far, back_send.at[0], back_recv.at[0], (other, before, tp)),
        remote(grad, back_near, back_send.at[1], back_recv.at[1], (rep, before, tp)),
    ]
    for copy in back:
        copy.start()

    loads[3].wait()
    loads[4].wait()

    def og_copy(j):
        rows = lanes(j)
        return remote(og.at[rows], og_recv.at[rows], og_ss.at[j], og_rs.at[j], (other, sec, tp))

    def outer_gradient(j, _):
        rows = lanes(j)
        weight_grad = lax.dot_general(
            normed[:, rows], gv[...], (((0,), (0,)), ((), ())), preferred_element_type=F32
        ) * scale
        local_new = w[rows, :].astype(F32) - inner_rate * weight_grad
        og[rows, :] = (a[rows, :].astype(F32) - local_new).astype(BF16)
        og_copy(j).start()
        return _

    lax.fori_loop(0, BLOCKS, outer_gradient, 0)

    out_row = lax.broadcasted_iota(jnp.int32, (PAD, TOK), 0)
    in_row = lax.broadcasted_iota(jnp.int32, (PAD, TOK), 1)
    place = lax.rem(out_row, ROWS)
    pick = jnp.where((in_row == (out_row // ROWS) * OWN + place) & (place < OWN), 1.0, 0.0)
    padded[...] = jnp.dot(pick.astype(BF16), normed[...], preferred_element_type=F32).astype(BF16)

    def partial_values(b, _):
        rows = pl.ds(pl.multiple_of(b * ROWS, ROWS), ROWS)
        vals[b] = jnp.dot(padded[rows, :], w[...], preferred_element_type=F32) * scale
        return _

    lax.fori_loop(0, 8, partial_values, 0)
    for z in range(4):
        vsend[z] = vals[2 * z + 1 - core].astype(BF16)
    core_copy = remote(vsend, vrecv, core_sem.at[0], core_sem.at[1], (rep, sec, sibling))
    core_copy.start()
    core_copy.wait()
    z_copies = []
    for d in range(1, 4):
        z = lax.rem(zlo + d, 4)
        zsend[d] = (vals[2 * z + core] + vrecv[z].astype(F32)).astype(BF16)
        copy = remote(zsend.at[d], zrecv.at[d], z_ss.at[d], z_rs.at[d], (rep, sec, 2 * z + core))
        copy.start()
        z_copies.append(copy)
    total = vals[2 * zlo + core] + vrecv[zlo].astype(F32)
    for d, copy in zip(range(1, 4), z_copies):
        copy.wait()
        total = total + zrecv[d].astype(F32)
    vout[...] = total.astype(BF16)
    val_copy = pltpu.make_async_copy(vout, val_out, out_sem.at[16])
    val_copy.start()

    paired = pair_mask[...] != 0

    def out_copies(j):
        rows = lanes(j)
        return (
            pltpu.make_async_copy(anc.at[rows], anc_out.at[rows], out_sem.at[j]),
            pltpu.make_async_copy(mom.at[rows], mom_out.at[rows], out_sem.at[j + 8]),
        )

    def outer_step(j, _):
        rows = lanes(j)
        og_copy(j).wait()
        own = og[rows, :].astype(F32)
        chosen = jnp.where(paired, og_recv[rows, :].astype(F32), own)
        mean_grad = 0.5 * (own + chosen)
        momentum_next = keep_rate * m[rows, :].astype(F32) + mean_grad
        anc[rows, :] = (
            a[rows, :].astype(F32) - outer_rate * (mean_grad + keep_rate * momentum_next)
        ).astype(BF16)
        mom[rows, :] = momentum_next.astype(BF16)
        for copy in out_copies(j):
            copy.start()
        return _

    lax.fori_loop(0, BLOCKS, outer_step, 0)

    for copy in back:
        copy.wait()
    back_take = back_mask[...] != 0

    def returned(j, _):
        cols = lanes(j)
        x = jnp.where(back_take, back_near[:, cols].astype(F32), back_far[:, cols].astype(F32))
        grad[:, cols] = x.astype(BF16)
        return _

    lax.fori_loop(0, BLOCKS, returned, 0)
    ret_copy = pltpu.make_async_copy(grad, ret_out, out_sem.at[17])
    ret_copy.start()

    def finish(j, _):
        for copy in out_copies(j):
            copy.wait()
        return _

    lax.fori_loop(0, BLOCKS, finish, 0)
    val_copy.wait()
    ret_copy.wait()


def on_device(
    upstream, norm_gain, grad_values, grad_other, local_weights, anchor, momentum,
    section_routes, pairing,
):
    section = lax.axis_index("section")
    replica = lax.axis_index("rep")

    def mask(value, width):
        return jnp.full((1, width), value.astype(jnp.int32))

    in_mask = mask(section_routes[(section + 15) % 16, replica] == replica, LANE)
    back_mask = mask(section_routes[section, replica] == replica, LANE)
    pair_mask = mask(pairing[section, replica] != replica, W)

    any_spec = pl.BlockSpec(memory_space=pl.ANY)
    vmem_spec = pl.BlockSpec(memory_space=pltpu.VMEM)
    dma = pltpu.SemaphoreType.DMA
    tokens = pltpu.VMEM((TOK, W), BF16)
    square = pltpu.VMEM((W, W), BF16)
    values, returned, anchor_new, momentum_new = pl.pallas_call(
        kernel,
        out_shape=(
            jax.ShapeDtypeStruct((ROWS, W), BF16),
            jax.ShapeDtypeStruct((TOK, W), BF16),
            jax.ShapeDtypeStruct((W, W), BF16),
            jax.ShapeDtypeStruct((W, W), BF16),
        ),
        in_specs=[any_spec, vmem_spec] + [any_spec] * 5 + [vmem_spec] * 3,
        out_specs=(any_spec,) * 4,
        scratch_shapes=[
            tokens, tokens, tokens, tokens, square, square, square,
            pltpu.VMEM((TOK, W), F32),
            tokens,
            pltpu.VMEM((PAD, W), BF16),
            pltpu.VMEM((2, PAD, LANE), F32),
            pltpu.VMEM((2, 8, PAD), F32),
            pltpu.VMEM((2, 8, 8, PAD), F32),
            pltpu.VMEM((TOK, LANE), F32),
            pltpu.VMEM((TOK, LANE), F32),
            tokens, tokens, tokens,
            square, square, square, square,
            pltpu.VMEM((8, ROWS, W), F32),
            pltpu.VMEM((4, ROWS, W), BF16),
            pltpu.VMEM((4, ROWS, W), BF16),
            pltpu.VMEM((4, ROWS, W), BF16),
            pltpu.VMEM((4, ROWS, W), BF16),
            pltpu.VMEM((ROWS, W), BF16),
            dma((5,)), dma((2,)), dma((2,)), dma((2,)), dma((2,)), dma((8,)), dma((8,)),
            dma((8,)), dma((8,)), dma((2,)), dma((4,)), dma((4,)), dma((18,)),
        ],
        compiler_params=pltpu.CompilerParams(
            collective_id=0, has_side_effects=True, vmem_limit_bytes=56 * 2**20
        ),
        cost_estimate=pl.CostEstimate(
            flops=6 * TOK * W * W, bytes_accessed=13 * 2**20, transcendentals=TOK * LANE
        ),
        name="layer",
    )(
        upstream[0, 0], norm_gain[None, :], grad_values[0, 0], grad_other[0, 0],
        local_weights[0, 0], anchor[0, 0], momentum[0, 0], in_mask, back_mask, pair_mask,
    )
    return (
        values[None, None, :OWN],
        returned[None, None],
        anchor_new[None, None],
        momentum_new[None, None],
    )


def solution(mesh):
    return jax.shard_map(
        on_device,
        mesh=mesh,
        in_specs=(
            P("rep", "section", None, "tp"),
            P("tp"),
            P("rep", "section", None, None),
            P("rep", "section", None, "tp"),
            P("rep", "section", "tp", None),
            P("rep", "section", "tp", None),
            P("rep", "section", "tp", None),
            P(),
            P(),
        ),
        out_specs=(
            P("rep", "section", "tp", None),
            P("rep", "section", None, "tp"),
            P("rep", "section", "tp", None),
            P("rep", "section", "tp", None),
        ),
        check_vma=False,
    )
```

```python
import functools

import jax
import jax.numpy as jnp
from jax import lax
from jax.experimental import pallas as pl
from jax.experimental.pallas import tpu as pltpu
from jax.sharding import PartitionSpec as P

MESH = pl.DeviceIdType.MESH
F32 = jnp.float32
BF16 = jnp.bfloat16

D = 8192
eps = 1e-05
inner_rate = 1.0
outer_rate = 0.7
keep_rate = 0.9
scale = D ** (-0.5)

TOK = 352
PAD = 384
OWN = 44
ROWS = 48
W = 1024
LANE = 128
BLOCKS = W // LANE
SECTIONS = 16
PHASES = 4
HALF = TOK // 2


def remote(src, dst, send_sem, recv_sem, device):
    return pltpu.make_async_remote_copy(
        src_ref=src, dst_ref=dst, send_sem=send_sem, recv_sem=recv_sem,
        device_id=device, device_id_type=MESH,
    )


def lanes(j):
    return pl.ds(pl.multiple_of(j * LANE, LANE), LANE)


def kernel(
    kp, kf,
    up_hbm, gain_ref, gv_hbm, go_hbm, w_hbm, a_hbm, m_hbm, flags_hbm,
    val_out, ret_out, anc_out, mom_out,
    near, far, gv, go, w, a, m, gn, normed, padded, parts, stat_send, stat_recv,
    inv_ref, dot_ref, grad, og, anc, mom, vals, vsend, vrecv, zsend, zrecv, vout,
    b_scat, b_slot, b_cross, b_turn, scat_a, scat_b, scat_c, scat_d, slot, cross_a, cross_b, cross_c, cross_d, turn, home, sel_p, rank_p, sel_f, rank_f, crosses,
    load_sem, fwd_send, fwd_recv, stat_ss, stat_rs, core_sem, z_ss, z_rs, out_sem,
    bs_ss, bs_rs, bx_sem, bt_ss, bt_rs, s_ss, s_rs, x_ss, x_rs, t_ss, t_rs,
):
    rep = lax.axis_index("rep")
    sec = lax.axis_index("section")
    tp = lax.axis_index("tp")
    core = lax.rem(tp, 2)
    zlo = tp // 2
    other = 1 - rep
    after = lax.rem(sec + 1, SECTIONS)
    before = lax.rem(sec + SECTIONS - 1, SECTIONS)
    sibling = 2 * zlo + 1 - core

    scat = (scat_a, scat_b, scat_c, scat_d)
    cross = (cross_a, cross_b, cross_c, cross_d)

    def column(d):
        return lax.rem(sec + d, SECTIONS)

    loads = [
        pltpu.make_async_copy(src, dst, load_sem.at[i])
        for i, (src, dst) in enumerate(
            [(gv_hbm, gv), (w_hbm, w), (go_hbm, go), (a_hbm, a), (m_hbm, m), (flags_hbm, crosses)]
        )
    ]
    for load in loads:
        load.start()

    barrier = pltpu.get_barrier_semaphore()
    peers = [(other, sec, tp), (other, after, tp), (other, before, tp)]
    peers += [(rep, column(d), tp) for d in range(1, SECTIONS)]
    peers += [(rep, sec, lax.rem(tp + d, 8)) for d in range(1, 8)]
    with jax.named_scope("entry"):
        for peer in peers:
            pl.semaphore_signal(barrier, inc=1, device_id=peer, device_id_type=MESH)
        pl.semaphore_wait(barrier, len(peers))

    fwd = [
        remote(up_hbm, far, fwd_send.at[0], fwd_recv.at[0], (other, after, tp)),
        remote(up_hbm, near, fwd_send.at[1], fwd_recv.at[1], (rep, after, tp)),
    ]
    for copy in fwd:
        copy.start()

    loads[5].wait()
    for first, sel, rank, count in ((0, sel_p, rank_p, kp), (SECTIONS, sel_f, rank_f, kf)):
        flags = [crosses[first + i] for i in range(SECTIONS)]
        seen = jnp.int32(0)
        chosen = [jnp.int32(0)] * count
        for i in range(SECTIONS):
            rank[i] = jnp.minimum(seen, count - 1)
            chosen = [
                jnp.where((flags[i] != 0) & (seen == k), i, chosen[k]) if k <= i else chosen[k]
                for k in range(count)
            ]
            seen = seen + flags[i]
        for k in range(count):
            sel[k] = chosen[k]

    for load in loads[:3]:
        load.wait()

    def grad_normed(j, _):
        cols = lanes(j)
        product = lax.dot_general(
            gv[...], w[cols, :], (((1,), (1,)), ((), ())), preferred_element_type=F32
        )
        gn[:, cols] = product * scale + go[:, cols].astype(F32)
        return _

    with jax.named_scope("grad_normed"):
        lax.fori_loop(0, BLOCKS, grad_normed, 0)
    parts[...] = jnp.zeros_like(parts)

    with jax.named_scope("arrive"):
        for copy in fwd:
            copy.wait()

    take_near = crosses[SECTIONS + before] == 0

    def statistics(j, _):
        cols = lanes(j)
        x = jnp.where(take_near, near[:, cols].astype(F32), far[:, cols].astype(F32))
        near[:, cols] = x.astype(BF16)
        parts[0, 0:TOK, :] += x * x
        parts[1, 0:TOK, :] += x * gain_ref[:, cols] * gn[:, cols]
        return _

    with jax.named_scope("statistics"):
        lax.fori_loop(0, BLOCKS, statistics, 0)

        ones = jnp.full((8, LANE), 1.0, F32)
        for i in range(2):
            row = lax.dot_general(
                ones, parts[i], (((1,), (1,)), ((), ())),
                preferred_element_type=F32, precision=lax.Precision.HIGHEST,
            )
            stat_send[i] = row
            stat_recv[i, 0] = row
    stat_copies = []
    for d in range(1, 8):
        copy = remote(
            stat_send, stat_recv.at[:, d], stat_ss.at[d], stat_rs.at[d],
            (rep, sec, lax.rem(tp + d, 8)),
        )
        copy.start()
        stat_copies.append(copy)
    with jax.named_scope("stat_wait"):
        for copy in stat_copies:
            copy.wait()

    def b_piece(j):
        return (pl.ds(pl.multiple_of((j // 8) * HALF, 16), HALF), lanes(lax.rem(j, 8)))

    def b_scatter(d):
        q = column(d)
        return remote(
            grad.at[b_piece(q)], b_scat.at[sec], bs_ss.at[d], bs_rs.at[d], (rep, q, tp)
        )

    def b_gather(d):
        q = column(d)
        return remote(
            b_turn.at[q], ret_out.at[b_piece(sec)], bt_ss.at[d], bt_rs.at[d], (rep, q, tp)
        )

    b_swap = remote(b_slot, b_cross, bx_sem.at[0], bx_sem.at[1], (other, sec, tp))

    def scatter(h, d):
        q = column(d)
        return remote(og.at[q, h], scat[h].at[sec], s_ss.at[h, d], s_rs.at[h, d], (rep, q, tp))

    def swap(h):
        return remote(slot.at[h], cross[h], x_ss.at[h], x_rs.at[h], (other, sec, tp))

    def gather(h, d):
        q = column(d)
        return remote(turn.at[h, q], home.at[h, sec], t_ss.at[h, d], t_rs.at[h, d], (rep, q, tp))

    def each(first, last, body):
        def step(i, _):
            body(i)
            return _

        lax.fori_loop(first, last, step, 0)

    with jax.named_scope("input_gradient"):
        eighth = jnp.full((64, LANE), 0.125, F32)
        sums = [
            lax.dot_general(
                stat_recv[i].reshape(64, PAD), eighth, (((0,), (0,)), ((), ())),
                preferred_element_type=F32, precision=lax.Precision.HIGHEST,
            )
            for i in range(2)
        ]
        inv = lax.rsqrt(sums[0][0:TOK] / D + eps)
        inv_ref[...] = inv
        dot_ref[...] = inv * inv * inv * sums[1][0:TOK] / D

        def input_gradient(j):
            cols = lanes(j)
            x = near[:, cols].astype(F32)
            gain = gain_ref[:, cols]
            inv = inv_ref[...]
            grad[:, cols] = (inv * gain * gn[:, cols] - x * dot_ref[...]).astype(BF16)
            normed[:, cols] = (x * inv * gain).astype(BF16)

        each(0, BLOCKS, input_gradient)
    each(1, SECTIONS, lambda d: b_scatter(d).start())
    mine = b_piece(sec)
    b_scat[sec] = grad[mine]

    loads[3].wait()
    loads[4].wait()

    def outer_gradient(i):
        c = lax.rem(sec // 2 + i, BLOCKS)
        rows = lanes(c)
        weight_grad = lax.dot_general(
            normed[:, rows], gv[...], (((0,), (0,)), ((), ())), preferred_element_type=F32
        ) * scale
        local_new = w[rows, :].astype(F32) - inner_rate * weight_grad
        anchor = a[pl.ds(2 * c, 2)].reshape(LANE, W).astype(F32)
        og[pl.ds(2 * c, 2)] = (anchor - local_new).astype(BF16).reshape(2, PHASES, 16, W)
        for e in range(2):
            d = lax.rem(2 * c + e - sec + SECTIONS, SECTIONS)

            @pl.when(d != 0)
            def _():
                scatter(0, d).start()

    with jax.named_scope("outer_gradient"):
        each(0, BLOCKS, outer_gradient)
    for h in range(PHASES):
        scat[h][sec] = og[sec, h]
    each(1, SECTIONS, lambda d: scatter(1, d).start())

    def cross_back():
        with jax.named_scope("back_scatter_wait"):
            each(1, SECTIONS, lambda d: b_scatter(d).wait_recv())

        def fill(k):
            b_slot[k] = b_scat[lax.rem(sel_f[k] + 1, SECTIONS)]

        each(0, kf, fill)
        b_swap.start()

    def turn_back():
        with jax.named_scope("back_cross_wait"):
            b_swap.wait_recv()

        def fill(i):
            flipped = crosses[SECTIONS + i] != 0
            crossed = b_cross[rank_f[i]].astype(F32)
            stayed = b_scat[lax.rem(i + 1, SECTIONS)].astype(F32)
            b_turn[i] = jnp.where(flipped, crossed, stayed).astype(BF16)

        each(0, SECTIONS, fill)
        each(1, SECTIONS, lambda d: b_gather(d).start())
        b_home.start()

    b_home = pltpu.make_async_copy(b_turn.at[sec], ret_out.at[mine], out_sem.at[9])

    def cross_out(h):
        with jax.named_scope("scatter_wait"):
            each(1, SECTIONS, lambda d: scatter(h, d).wait_recv())

        def fill(k):
            slot[h, k] = scat[h][sel_p[k]]

        each(0, kp, fill)
        swap(h).start()

    def turn_out(h):
        with jax.named_scope("cross_wait"):
            swap(h).wait_recv()

        def fill(i):
            turn[h, i] = cross[h][rank_p[i]]

        each(0, SECTIONS, fill)
        each(1, SECTIONS, lambda d: gather(h, d).start())
        home[h, sec] = turn[h, sec]

    paired = crosses[sec] != 0

    def out_copies(h):
        return (
            pltpu.make_async_copy(anc.at[:, h], anc_out.at[:, h], out_sem.at[h]),
            pltpu.make_async_copy(mom.at[:, h], mom_out.at[:, h], out_sem.at[h + PHASES]),
        )

    def outer_step(h):
        with jax.named_scope("gather_wait"):
            each(1, SECTIONS, lambda d: gather(h, d).wait_recv())

        def step(j):
            own = og[j, h].astype(F32)
            chosen = jnp.where(paired, home[h, j].astype(F32), own)
            mean_grad = 0.5 * (own + chosen)
            momentum_next = keep_rate * m[j, h].astype(F32) + mean_grad
            anc[j, h] = (
                a[j, h].astype(F32) - outer_rate * (mean_grad + keep_rate * momentum_next)
            ).astype(BF16)
            mom[j, h] = momentum_next.astype(BF16)

        with jax.named_scope("outer_step"):
            each(0, SECTIONS, step)
        for copy in out_copies(h):
            copy.start()

    cross_back()
    cross_out(0)
    each(1, SECTIONS, lambda d: scatter(2, d).start())

    with jax.named_scope("values"):
        out_row = lax.broadcasted_iota(jnp.int32, (PAD, TOK), 0)
        in_row = lax.broadcasted_iota(jnp.int32, (PAD, TOK), 1)
        place = lax.rem(out_row, ROWS)
        pick = jnp.where((in_row == (out_row // ROWS) * OWN + place) & (place < OWN), 1.0, 0.0)
        padded[...] = jnp.dot(
            pick.astype(BF16), normed[...], preferred_element_type=F32
        ).astype(BF16)

        def partial_values(b):
            rows = pl.ds(pl.multiple_of(b * ROWS, ROWS), ROWS)
            vals[b] = jnp.dot(padded[rows, :], w[...], preferred_element_type=F32) * scale

        each(0, 8, partial_values)
        for z in range(4):
            vsend[z] = vals[2 * z + 1 - core].astype(BF16)
        core_copy = remote(vsend, vrecv, core_sem.at[0], core_sem.at[1], (rep, sec, sibling))
        core_copy.start()
        core_copy.wait()
        z_copies = []
        for d in range(1, 4):
            z = lax.rem(zlo + d, 4)
            zsend[d] = (vals[2 * z + core] + vrecv[z].astype(F32)).astype(BF16)
            copy = remote(
                zsend.at[d], zrecv.at[d], z_ss.at[d], z_rs.at[d], (rep, sec, 2 * z + core)
            )
            copy.start()
            z_copies.append(copy)

    cross_out(1)
    each(1, SECTIONS, lambda d: scatter(3, d).start())
    turn_back()
    cross_out(2)
    turn_out(0)
    cross_out(3)
    turn_out(1)

    total = vals[2 * zlo + core] + vrecv[zlo].astype(F32)
    with jax.named_scope("values_wait"):
        for d, copy in zip(range(1, 4), z_copies):
            copy.wait()
            total = total + zrecv[d].astype(F32)
    vout[...] = total.astype(BF16)
    val_copy = pltpu.make_async_copy(vout, val_out, out_sem.at[8])
    val_copy.start()

    outer_step(0)
    turn_out(2)
    outer_step(1)
    turn_out(3)
    outer_step(2)
    with jax.named_scope("back_gather_wait"):
        each(1, SECTIONS, lambda d: b_gather(d).wait_recv())
    outer_step(3)

    with jax.named_scope("finish"):
        b_swap.wait_send()
        for h in range(PHASES):
            swap(h).wait_send()

        def sent(d):
            b_scatter(d).wait_send()
            b_gather(d).wait_send()
            for h in range(PHASES):
                scatter(h, d).wait_send()
                gather(h, d).wait_send()

        each(1, SECTIONS, sent)
        b_home.wait()
        val_copy.wait()
        for h in range(PHASES):
            for copy in out_copies(h):
                copy.wait()


def finish_kernel(val, ret, anc, mom, val_out, ret_out, anc_out, mom_out, *scratch):
    into, out = scratch[-2:]
    parts = []
    for src, held, dst, cuts in zip(
        (anc, mom, ret), scratch[:3], (anc_out, mom_out, ret_out), (4, 4, 2)
    ):
        size = held.shape[0] // cuts
        for i in range(cuts):
            rows = pl.ds(i * size, size)
            n = len(parts)
            parts.append((
                pltpu.make_async_copy(src.at[rows], held.at[rows], into.at[n]),
                pltpu.make_async_copy(held.at[rows], dst.at[rows], out.at[n]),
            ))
    for first, _ in parts:
        first.start()
    val_out[...] = val[0:OWN, :]
    for first, second in parts:
        first.wait()
        second.start()
    for _, second in parts:
        second.wait()


def layer(kp, kf, collective_id, *args):
    any_spec = pl.BlockSpec(memory_space=pl.ANY)
    vmem_spec = pl.BlockSpec(memory_space=pltpu.VMEM)
    dma = pltpu.SemaphoreType.DMA
    tokens = pltpu.VMEM((TOK, W), BF16)
    square = pltpu.VMEM((W, W), BF16)
    cut = pltpu.VMEM((SECTIONS, PHASES, 16, W), BF16)
    table = pltpu.SMEM((SECTIONS,), jnp.int32)

    def pieces(count):
        return pltpu.VMEM((count, HALF, LANE), BF16)

    def rows(count):
        return pltpu.VMEM((count, 16, W), BF16)

    def slots(count):
        return pltpu.VMEM((PHASES, count, 16, W), BF16)

    return pl.pallas_call(
        functools.partial(kernel, kp, kf),
        out_shape=(
            jax.ShapeDtypeStruct((ROWS, W), BF16),
            jax.ShapeDtypeStruct((TOK, W), BF16),
            jax.ShapeDtypeStruct((SECTIONS, PHASES, 16, W), BF16),
            jax.ShapeDtypeStruct((SECTIONS, PHASES, 16, W), BF16),
        ),
        in_specs=[any_spec, vmem_spec] + [any_spec] * 6,
        out_specs=(any_spec,) * 4,
        scratch_shapes=[
            tokens, tokens, tokens, tokens, square, cut, cut,
            pltpu.VMEM((TOK, W), F32),
            tokens,
            pltpu.VMEM((PAD, W), BF16),
            pltpu.VMEM((2, PAD, LANE), F32),
            pltpu.VMEM((2, 8, PAD), F32),
            pltpu.VMEM((2, 8, 8, PAD), F32),
            pltpu.VMEM((TOK, LANE), F32),
            pltpu.VMEM((TOK, LANE), F32),
            tokens,
            cut, cut, cut,
            pltpu.VMEM((8, ROWS, W), F32),
            pltpu.VMEM((4, ROWS, W), BF16),
            pltpu.VMEM((4, ROWS, W), BF16),
            pltpu.VMEM((4, ROWS, W), BF16),
            pltpu.VMEM((4, ROWS, W), BF16),
            pltpu.VMEM((ROWS, W), BF16),
            pieces(SECTIONS), pieces(kf), pieces(kf), pieces(SECTIONS),
            *[rows(SECTIONS)] * 4, slots(kp), *[rows(kp)] * 4, slots(SECTIONS), slots(SECTIONS),
            table, table, table, table, pltpu.SMEM((2 * SECTIONS,), jnp.int32),
            dma((6,)), dma((2,)), dma((2,)), dma((8,)), dma((8,)), dma((2,)), dma((4,)), dma((4,)),
            dma((10,)),
            dma((SECTIONS,)), dma((SECTIONS,)), dma((2,)), dma((SECTIONS,)), dma((SECTIONS,)),
            dma((PHASES, SECTIONS)), dma((PHASES, SECTIONS)), dma((PHASES,)), dma((PHASES,)),
            dma((PHASES, SECTIONS)), dma((PHASES, SECTIONS)),
        ],
        compiler_params=pltpu.CompilerParams(
            collective_id=collective_id, has_side_effects=True, vmem_limit_bytes=56 * 2**20
        ),
        cost_estimate=pl.CostEstimate(
            flops=6 * TOK * W * W, bytes_accessed=13 * 2**20, transcendentals=TOK * LANE
        ),
        name="layer",
    )(*args)


ROOM = ((8, 11), (10, 11), (16, 16))


def on_device(
    upstream, norm_gain, grad_values, grad_other, local_weights, anchor, momentum,
    section_routes, pairing,
):
    cut = (SECTIONS, PHASES, 16, W)
    flags = jnp.concatenate([pairing[:, 0], section_routes[:, 0]])
    args = (
        upstream[0, 0], norm_gain[None, :], grad_values[0, 0], grad_other[0, 0],
        local_weights[0, 0], anchor.reshape(cut), momentum.reshape(cut), flags,
    )
    crossing = jnp.sum(flags.reshape(2, SECTIONS), axis=1)
    branch = jnp.int32(0)
    for kp, kf in ROOM[:-1]:
        branch += ((crossing[0] > kp) | (crossing[1] > kf)).astype(jnp.int32)
    outs = lax.switch(
        branch, [functools.partial(layer, kp, kf, i) for i, (kp, kf) in enumerate(ROOM)], *args
    )
    any_spec = pl.BlockSpec(memory_space=pl.ANY)
    vmem_spec = pl.BlockSpec(memory_space=pltpu.VMEM)
    values, returned, anchor_new, momentum_new = pl.pallas_call(
        finish_kernel,
        out_shape=(
            jax.ShapeDtypeStruct((OWN, W), BF16),
            jax.ShapeDtypeStruct((TOK, W), BF16),
            jax.ShapeDtypeStruct(cut, BF16),
            jax.ShapeDtypeStruct(cut, BF16),
        ),
        in_specs=[vmem_spec] + [any_spec] * 3,
        out_specs=(vmem_spec,) + (any_spec,) * 3,
        scratch_shapes=[
            pltpu.VMEM(cut, BF16), pltpu.VMEM(cut, BF16), pltpu.VMEM((TOK, W), BF16),
            pltpu.SemaphoreType.DMA((10,)), pltpu.SemaphoreType.DMA((10,)),
        ],
        compiler_params=pltpu.CompilerParams(vmem_limit_bytes=32 * 2**20),
        name="finish",
    )(*outs)
    return (
        values[None, None],
        returned[None, None],
        anchor_new.reshape(1, 1, W, W),
        momentum_new.reshape(1, 1, W, W),
    )


def solution(mesh):
    return jax.shard_map(
        on_device,
        mesh=mesh,
        in_specs=(
            P("rep", "section", None, "tp"),
            P("tp"),
            P("rep", "section", None, None),
            P("rep", "section", None, "tp"),
            P("rep", "section", "tp", None),
            P("rep", "section", "tp", None),
            P("rep", "section", "tp", None),
            P(),
            P(),
        ),
        out_specs=(
            P("rep", "section", "tp", None),
            P("rep", "section", None, "tp"),
            P("rep", "section", "tp", None),
            P("rep", "section", "tp", None),
        ),
        check_vma=False,
    )
```

```python
import functools

import jax
import jax.numpy as jnp
from jax import lax
from jax.experimental import pallas as pl
from jax.experimental.pallas import tpu as pltpu
from jax.sharding import PartitionSpec as P

MESH = pl.DeviceIdType.MESH
F32 = jnp.float32
BF16 = jnp.bfloat16

D = 8192
eps = 1e-05
inner_rate = 1.0
outer_rate = 0.7
keep_rate = 0.9
scale = D ** (-0.5)

TOK = 352
PAD = 384
OWN = 44
ROWS = 48
W = 1024
LANE = 128
BLOCKS = W // LANE
SECTIONS = 16
PHASES = 4
HALF = TOK // 2
WIDE = 256


def remote(src, dst, send_sem, recv_sem, device):
    return pltpu.make_async_remote_copy(
        src_ref=src, dst_ref=dst, send_sem=send_sem, recv_sem=recv_sem,
        device_id=device, device_id_type=MESH,
    )


def lanes(j):
    return pl.ds(pl.multiple_of(j * LANE, LANE), LANE)


def kernel(
    kp, kf,
    up_hbm, gain_ref, gv_hbm, go_hbm, w_hbm, a_hbm, m_hbm, flags_hbm,
    val_out, ret_out, anc_out, mom_out,
    near, far, gv, go, w, a, m, gn, normed, padded, parts, stat_send, stat_recv,
    inv_ref, dot_ref, grad, og, anc, mom, vals, vsend, vrecv, zsend, zrecv, vout,
    b_scat, b_slot, b_cross, b_turn, scat_a, scat_b, scat_c, scat_d, slot, cross_a, cross_b, cross_c, cross_d, turn, home, sel_p, rank_p, sel_f, rank_f, crosses,
    load_sem, fwd_send, fwd_recv, stat_sem, core_sem, z_sem, out_sem,
    bs_sem, bx_sem, bt_sem, s_ss, s_rs, x_ss, x_rs, t_ss, t_rs,
):
    rep = lax.axis_index("rep")
    sec = lax.axis_index("section")
    tp = lax.axis_index("tp")
    core = lax.rem(tp, 2)
    zlo = tp // 2
    other = 1 - rep
    after = lax.rem(sec + 1, SECTIONS)
    before = lax.rem(sec + SECTIONS - 1, SECTIONS)
    sibling = 2 * zlo + 1 - core

    scat = (scat_a, scat_b, scat_c, scat_d)
    cross = (cross_a, cross_b, cross_c, cross_d)

    def column(d):
        return lax.rem(sec + d, SECTIONS)

    loads = [
        pltpu.make_async_copy(src, dst, load_sem.at[i])
        for i, (src, dst) in enumerate(
            [(gv_hbm, gv), (w_hbm, w), (go_hbm, go), (a_hbm, a), (m_hbm, m), (flags_hbm, crosses)]
        )
    ]
    for load in loads:
        load.start()

    barrier = pltpu.get_barrier_semaphore()
    peers = [(other, sec, tp), (other, after, tp), (other, before, tp)]
    peers += [(rep, column(d), tp) for d in range(1, SECTIONS)]
    peers += [(rep, sec, lax.rem(tp + d, 8)) for d in range(1, 8)]
    with jax.named_scope("entry"):
        for peer in peers:
            pl.semaphore_signal(barrier, inc=1, device_id=peer, device_id_type=MESH)
        pl.semaphore_wait(barrier, len(peers))

    fwd = [
        remote(up_hbm, far, fwd_send.at[0], fwd_recv.at[0], (other, after, tp)),
        remote(up_hbm, near, fwd_send.at[1], fwd_recv.at[1], (rep, after, tp)),
    ]
    for copy in fwd:
        copy.start()

    loads[5].wait()
    for first, sel, rank, count in ((0, sel_p, rank_p, kp), (SECTIONS, sel_f, rank_f, kf)):
        flags = [crosses[first + i] for i in range(SECTIONS)]
        seen = jnp.int32(0)
        chosen = [jnp.int32(0)] * count
        for i in range(SECTIONS):
            rank[i] = jnp.minimum(seen, count - 1)
            chosen = [
                jnp.where((flags[i] != 0) & (seen == k), i, chosen[k]) if k <= i else chosen[k]
                for k in range(count)
            ]
            seen = seen + flags[i]
        for k in range(count):
            sel[k] = chosen[k]

    for load in loads[:3]:
        load.wait()

    def grad_normed(j, _):
        cols = pl.ds(pl.multiple_of(j * WIDE, WIDE), WIDE)
        product = lax.dot_general(
            gv[...], w[cols, :], (((1,), (1,)), ((), ())), preferred_element_type=F32
        )
        gn[:, cols] = product * scale + go[:, cols].astype(F32)
        return _

    with jax.named_scope("grad_normed"):
        lax.fori_loop(0, W // WIDE, grad_normed, 0)
    parts[...] = jnp.zeros_like(parts)

    with jax.named_scope("arrive"):
        for copy in fwd:
            copy.wait()

    take_near = crosses[SECTIONS + before] == 0

    def statistics(j, _):
        cols = lanes(j)
        x = jnp.where(take_near, near[:, cols].astype(F32), far[:, cols].astype(F32))
        near[:, cols] = x.astype(BF16)
        parts[0, 0:TOK, :] += x * x
        parts[1, 0:TOK, :] += x * gain_ref[:, cols] * gn[:, cols]
        return _

    with jax.named_scope("statistics"):
        lax.fori_loop(0, BLOCKS, statistics, 0)

        ones = jnp.full((8, LANE), 1.0, F32)
        for i in range(2):
            row = lax.dot_general(
                ones, parts[i], (((1,), (1,)), ((), ())),
                preferred_element_type=F32, precision=lax.Precision.HIGHEST,
            )
            stat_send[i] = row
            stat_recv[i, 0] = row
    for d in range(1, 8):
        remote(
            stat_send, stat_recv.at[:, d], stat_sem.at[0], stat_sem.at[1],
            (rep, sec, lax.rem(tp + d, 8)),
        ).start()
    stat_all = remote(
        stat_recv.at[:, pl.ds(1, 7)], stat_recv.at[:, pl.ds(1, 7)],
        stat_sem.at[0], stat_sem.at[1], (other, sec, tp),
    )
    with jax.named_scope("stat_wait"):
        stat_all.wait()

    def b_piece(j):
        return (pl.ds(pl.multiple_of((j // 8) * HALF, 16), HALF), lanes(lax.rem(j, 8)))

    def b_scatter(d):
        q = column(d)
        return remote(
            grad.at[b_piece(q)], b_scat.at[sec], bs_sem.at[0], bs_sem.at[1], (rep, q, tp)
        )

    def b_gather(d):
        q = column(d)
        return remote(
            b_turn.at[q], ret_out.at[b_piece(sec)], bt_sem.at[0], bt_sem.at[1], (rep, q, tp)
        )

    def every(buffer, send_sem, recv_sem):
        ref = buffer.at[pl.ds(0, SECTIONS - 1)]
        return remote(ref, ref, send_sem, recv_sem, (other, sec, tp))

    b_scatter_all = every(b_scat, bs_sem.at[0], bs_sem.at[1])
    b_gather_all = every(b_turn, bt_sem.at[0], bt_sem.at[1])
    scatter_all = [every(scat[h], s_ss.at[h], s_rs.at[h]) for h in range(PHASES)]
    gather_all = [every(home.at[h], t_ss.at[h], t_rs.at[h]) for h in range(PHASES)]
    b_swap = remote(b_slot, b_cross, bx_sem.at[0], bx_sem.at[1], (other, sec, tp))

    def scatter(h, d):
        q = column(d)
        return remote(og.at[q, h], scat[h].at[sec], s_ss.at[h], s_rs.at[h], (rep, q, tp))

    def swap(h):
        return remote(slot.at[h], cross[h], x_ss.at[h], x_rs.at[h], (other, sec, tp))

    def gather(h, d):
        q = column(d)
        return remote(turn.at[h, q], home.at[h, sec], t_ss.at[h], t_rs.at[h], (rep, q, tp))

    def each(first, last, body):
        def step(i, _):
            body(i)
            return _

        lax.fori_loop(first, last, step, 0)

    with jax.named_scope("input_gradient"):
        eighth = jnp.full((64, LANE), 0.125, F32)
        sums = [
            lax.dot_general(
                stat_recv[i].reshape(64, PAD), eighth, (((0,), (0,)), ((), ())),
                preferred_element_type=F32, precision=lax.Precision.HIGHEST,
            )
            for i in range(2)
        ]
        inv = lax.rsqrt(sums[0][0:TOK] / D + eps)
        inv_ref[...] = inv
        dot_ref[...] = inv * inv * inv * sums[1][0:TOK] / D

        def input_gradient(j):
            cols = lanes(j)
            x = near[:, cols].astype(F32)
            gain = gain_ref[:, cols]
            inv = inv_ref[...]
            grad[:, cols] = (inv * gain * gn[:, cols] - x * dot_ref[...]).astype(BF16)
            normed[:, cols] = (x * inv * gain).astype(BF16)

        each(0, BLOCKS, input_gradient)
    each(1, SECTIONS, lambda d: b_scatter(d).start())
    mine = b_piece(sec)
    b_scat[sec] = grad[mine]

    with jax.named_scope("values"):
        out_row = lax.broadcasted_iota(jnp.int32, (PAD, TOK), 0)
        in_row = lax.broadcasted_iota(jnp.int32, (PAD, TOK), 1)
        place = lax.rem(out_row, ROWS)
        pick = jnp.where((in_row == (out_row // ROWS) * OWN + place) & (place < OWN), 1.0, 0.0)
        padded[...] = jnp.dot(
            pick.astype(BF16), normed[...], preferred_element_type=F32
        ).astype(BF16)

        def partial_values(j):
            cols = pl.ds(pl.multiple_of(j * WIDE, WIDE), WIDE)
            product = jnp.dot(padded[...], w[:, cols], preferred_element_type=F32) * scale
            vals[:, :, cols] = product.reshape(8, ROWS, WIDE)

        each(0, W // WIDE, partial_values)
        for z in range(4):
            vsend[z] = vals[2 * z + 1 - core].astype(BF16)
        core_copy = remote(vsend, vrecv, core_sem.at[0], core_sem.at[1], (rep, sec, sibling))
        core_copy.start()

    loads[3].wait()
    loads[4].wait()

    def outer_gradient(i):
        c = lax.rem(sec // 2 + i, BLOCKS)
        rows = lanes(c)
        weight_grad = lax.dot_general(
            normed[:, rows], gv[...], (((0,), (0,)), ((), ())), preferred_element_type=F32
        ) * scale
        local_new = w[rows, :].astype(F32) - inner_rate * weight_grad
        anchor = a[pl.ds(2 * c, 2)].reshape(LANE, W).astype(F32)
        og[pl.ds(2 * c, 2)] = (anchor - local_new).astype(BF16).reshape(2, PHASES, 16, W)
        for e in range(2):
            d = lax.rem(2 * c + e - sec + SECTIONS, SECTIONS)

            @pl.when(d != 0)
            def _():
                scatter(0, d).start()

    with jax.named_scope("outer_gradient"):
        each(0, BLOCKS, outer_gradient)
    for h in range(PHASES):
        scat[h][sec] = og[sec, h]
    with jax.named_scope("values_send"):
        core_copy.wait()
        for d in range(1, 4):
            z = lax.rem(zlo + d, 4)
            zsend[d] = (vals[2 * z + core] + vrecv[z].astype(F32)).astype(BF16)
            remote(
                zsend.at[d], zrecv.at[d], z_sem.at[0], z_sem.at[1], (rep, sec, 2 * z + core)
            ).start()
    z_all = remote(
        zrecv.at[pl.ds(1, 3)], zrecv.at[pl.ds(1, 3)], z_sem.at[0], z_sem.at[1], (other, sec, tp)
    )
    each(1, SECTIONS, lambda d: scatter(1, d).start())

    def cross_back():
        with jax.named_scope("back_scatter_wait"):
            b_scatter_all.wait_recv()

        def fill(k):
            b_slot[k] = b_scat[lax.rem(sel_f[k] + 1, SECTIONS)]

        each(0, kf, fill)
        b_swap.start()

    def turn_back():
        def fill(i):
            flipped = crosses[SECTIONS + i] != 0
            crossed = b_cross[rank_f[i]].astype(F32)
            stayed = b_scat[lax.rem(i + 1, SECTIONS)].astype(F32)
            b_turn[i] = jnp.where(flipped, crossed, stayed).astype(BF16)

        each(0, SECTIONS, fill)
        each(1, SECTIONS, lambda d: b_gather(d).start())
        b_home.start()

    b_home = pltpu.make_async_copy(b_turn.at[sec], ret_out.at[mine], out_sem.at[9])

    def cross_out(h):
        with jax.named_scope("scatter_wait"):
            scatter_all[h].wait_recv()

        def fill(k):
            slot[h, k] = scat[h][sel_p[k]]

        each(0, kp, fill)
        swap(h).start()

    def crossed_out(h):
        with jax.named_scope("cross_wait"):
            swap(h).wait_recv()

    def turn_out(h):
        def fill(i):
            turn[h, i] = cross[h][rank_p[i]]

        each(0, SECTIONS, fill)
        each(1, SECTIONS, lambda d: gather(h, d).start())
        home[h, sec] = turn[h, sec]

    paired = crosses[sec] != 0

    def out_copies(h):
        return (
            pltpu.make_async_copy(anc.at[:, h], anc_out.at[:, h], out_sem.at[h]),
            pltpu.make_async_copy(mom.at[:, h], mom_out.at[:, h], out_sem.at[h + PHASES]),
        )

    def outer_step(h):
        with jax.named_scope("gather_wait"):
            gather_all[h].wait_recv()

        def step(j):
            own = og[j, h].astype(F32)
            chosen = jnp.where(paired, home[h, j].astype(F32), own)
            mean_grad = 0.5 * (own + chosen)
            momentum_next = keep_rate * m[j, h].astype(F32) + mean_grad
            anc[j, h] = (
                a[j, h].astype(F32) - outer_rate * (mean_grad + keep_rate * momentum_next)
            ).astype(BF16)
            mom[j, h] = momentum_next.astype(BF16)

        with jax.named_scope("outer_step"):
            each(0, SECTIONS, step)
        for copy in out_copies(h):
            copy.start()

    cross_back()
    cross_out(0)
    each(1, SECTIONS, lambda d: scatter(2, d).start())

    with jax.named_scope("back_cross_wait"):
        b_swap.wait_recv()
    cross_out(1)
    turn_back()
    each(1, SECTIONS, lambda d: scatter(3, d).start())
    crossed_out(0)
    cross_out(2)
    turn_out(0)
    crossed_out(1)
    cross_out(3)
    turn_out(1)
    outer_step(0)
    crossed_out(2)
    turn_out(2)
    outer_step(1)
    crossed_out(3)
    turn_out(3)
    outer_step(2)
    total = vals[2 * zlo + core] + vrecv[zlo].astype(F32)
    with jax.named_scope("values_wait"):
        z_all.wait()
    for d in range(1, 4):
        total = total + zrecv[d].astype(F32)
    vout[...] = total.astype(BF16)
    val_copy = pltpu.make_async_copy(vout, val_out, out_sem.at[8])
    val_copy.start()


    with jax.named_scope("back_gather_wait"):
        b_gather_all.wait_recv()
    outer_step(3)

    with jax.named_scope("finish"):
        b_swap.wait_send()
        for h in range(PHASES):
            swap(h).wait_send()

        for copy in [b_scatter_all, b_gather_all] + scatter_all + gather_all:
            copy.wait_send()
        b_home.wait()
        val_copy.wait()
        for h in range(PHASES):
            for copy in out_copies(h):
                copy.wait()


def finish_kernel(val, ret, anc, mom, val_out, ret_out, anc_out, mom_out, *scratch):
    into, out = scratch[-2:]
    parts = []
    for src, held, dst, cuts in zip(
        (anc, mom, ret), scratch[:3], (anc_out, mom_out, ret_out), (4, 4, 2)
    ):
        size = held.shape[0] // cuts
        for i in range(cuts):
            rows = pl.ds(i * size, size)
            n = len(parts)
            parts.append((
                pltpu.make_async_copy(src.at[rows], held.at[rows], into.at[n]),
                pltpu.make_async_copy(held.at[rows], dst.at[rows], out.at[n]),
            ))
    for first, _ in parts:
        first.start()
    val_out[...] = val[0:OWN, :]
    for first, second in parts:
        first.wait()
        second.start()
    for _, second in parts:
        second.wait()


def layer(kp, kf, collective_id, *args):
    any_spec = pl.BlockSpec(memory_space=pl.ANY)
    vmem_spec = pl.BlockSpec(memory_space=pltpu.VMEM)
    dma = pltpu.SemaphoreType.DMA
    tokens = pltpu.VMEM((TOK, W), BF16)
    square = pltpu.VMEM((W, W), BF16)
    cut = pltpu.VMEM((SECTIONS, PHASES, 16, W), BF16)
    table = pltpu.SMEM((SECTIONS,), jnp.int32)

    def pieces(count):
        return pltpu.VMEM((count, HALF, LANE), BF16)

    def rows(count):
        return pltpu.VMEM((count, 16, W), BF16)

    def slots(count):
        return pltpu.VMEM((PHASES, count, 16, W), BF16)

    return pl.pallas_call(
        functools.partial(kernel, kp, kf),
        out_shape=(
            jax.ShapeDtypeStruct((ROWS, W), BF16),
            jax.ShapeDtypeStruct((TOK, W), BF16),
            jax.ShapeDtypeStruct((SECTIONS, PHASES, 16, W), BF16),
            jax.ShapeDtypeStruct((SECTIONS, PHASES, 16, W), BF16),
        ),
        in_specs=[any_spec, vmem_spec] + [any_spec] * 6,
        out_specs=(any_spec,) * 4,
        scratch_shapes=[
            tokens, tokens, tokens, tokens, square, cut, cut,
            pltpu.VMEM((TOK, W), F32),
            tokens,
            pltpu.VMEM((PAD, W), BF16),
            pltpu.VMEM((2, PAD, LANE), F32),
            pltpu.VMEM((2, 8, PAD), F32),
            pltpu.VMEM((2, 8, 8, PAD), F32),
            pltpu.VMEM((TOK, LANE), F32),
            pltpu.VMEM((TOK, LANE), F32),
            tokens,
            cut, cut, cut,
            pltpu.VMEM((8, ROWS, W), F32),
            pltpu.VMEM((4, ROWS, W), BF16),
            pltpu.VMEM((4, ROWS, W), BF16),
            pltpu.VMEM((4, ROWS, W), BF16),
            pltpu.VMEM((4, ROWS, W), BF16),
            pltpu.VMEM((ROWS, W), BF16),
            pieces(SECTIONS), pieces(kf), pieces(kf), pieces(SECTIONS),
            *[rows(SECTIONS)] * 4, slots(kp), *[rows(kp)] * 4, slots(SECTIONS), slots(SECTIONS),
            table, table, table, table, pltpu.SMEM((2 * SECTIONS,), jnp.int32),
            dma((6,)), dma((2,)), dma((2,)), dma((2,)), dma((2,)), dma((2,)), dma((10,)),
            dma((2,)), dma((2,)), dma((2,)),
            dma((PHASES,)), dma((PHASES,)), dma((PHASES,)), dma((PHASES,)), dma((PHASES,)), dma((PHASES,)),
        ],
        compiler_params=pltpu.CompilerParams(
            collective_id=collective_id, has_side_effects=True, vmem_limit_bytes=56 * 2**20
        ),
        cost_estimate=pl.CostEstimate(
            flops=6 * TOK * W * W, bytes_accessed=13 * 2**20, transcendentals=TOK * LANE
        ),
        name="layer",
    )(*args)


ROOM = ((8, 11), (10, 11), (16, 16))


def on_device(
    upstream, norm_gain, grad_values, grad_other, local_weights, anchor, momentum,
    section_routes, pairing,
):
    cut = (SECTIONS, PHASES, 16, W)
    flags = jnp.concatenate([pairing[:, 0], section_routes[:, 0]])
    args = (
        upstream[0, 0], norm_gain[None, :], grad_values[0, 0], grad_other[0, 0],
        local_weights[0, 0], anchor.reshape(cut), momentum.reshape(cut), flags,
    )
    crossing = jnp.sum(flags.reshape(2, SECTIONS), axis=1)
    branch = jnp.int32(0)
    for kp, kf in ROOM[:-1]:
        branch += ((crossing[0] > kp) | (crossing[1] > kf)).astype(jnp.int32)
    outs = lax.switch(
        branch, [functools.partial(layer, kp, kf, i) for i, (kp, kf) in enumerate(ROOM)], *args
    )
    any_spec = pl.BlockSpec(memory_space=pl.ANY)
    vmem_spec = pl.BlockSpec(memory_space=pltpu.VMEM)
    values, returned, anchor_new, momentum_new = pl.pallas_call(
        finish_kernel,
        out_shape=(
            jax.ShapeDtypeStruct((OWN, W), BF16),
            jax.ShapeDtypeStruct((TOK, W), BF16),
            jax.ShapeDtypeStruct(cut, BF16),
            jax.ShapeDtypeStruct(cut, BF16),
        ),
        in_specs=[vmem_spec] + [any_spec] * 3,
        out_specs=(vmem_spec,) + (any_spec,) * 3,
        scratch_shapes=[
            pltpu.VMEM(cut, BF16), pltpu.VMEM(cut, BF16), pltpu.VMEM((TOK, W), BF16),
            pltpu.SemaphoreType.DMA((10,)), pltpu.SemaphoreType.DMA((10,)),
        ],
        compiler_params=pltpu.CompilerParams(vmem_limit_bytes=32 * 2**20),
        name="finish",
    )(*outs)
    return (
        values[None, None],
        returned[None, None],
        anchor_new.reshape(1, 1, W, W),
        momentum_new.reshape(1, 1, W, W),
    )


def solution(mesh):
    return jax.shard_map(
        on_device,
        mesh=mesh,
        in_specs=(
            P("rep", "section", None, "tp"),
            P("tp"),
            P("rep", "section", None, None),
            P("rep", "section", None, "tp"),
            P("rep", "section", "tp", None),
            P("rep", "section", "tp", None),
            P("rep", "section", "tp", None),
            P(),
            P(),
        ),
        out_specs=(
            P("rep", "section", "tp", None),
            P("rep", "section", None, "tp"),
            P("rep", "section", "tp", None),
            P("rep", "section", "tp", None),
        ),
        check_vma=False,
    )
```

```python
import functools

import jax
import jax.numpy as jnp
from jax import lax
from jax.experimental import pallas as pl
from jax.experimental.pallas import tpu as pltpu
from jax.sharding import PartitionSpec as P

MESH = pl.DeviceIdType.MESH
F32 = jnp.float32
BF16 = jnp.bfloat16

D = 8192
eps = 1e-05
inner_rate = 1.0
outer_rate = 0.7
keep_rate = 0.9
scale = D ** (-0.5)

TOK = 352
PAD = 384
OWN = 44
ROWS = 48
W = 1024
LANE = 128
BLOCKS = W // LANE
SECTIONS = 16
STRIPS = 4
PHASES = 8
WIDTH = W // 2
STRAIGHT = 128
HALF = (TOK - STRAIGHT) // 2
WIDE = 256


def remote(src, dst, send_sem, recv_sem, device):
    return pltpu.make_async_remote_copy(
        src_ref=src, dst_ref=dst, send_sem=send_sem, recv_sem=recv_sem,
        device_id=device, device_id_type=MESH,
    )


def lanes(j):
    return pl.ds(pl.multiple_of(j * LANE, LANE), LANE)


def kernel(
    kp, kf,
    up_hbm, gain_ref, gv_hbm, go_hbm, w_hbm, a_hbm, m_hbm, flags_hbm,
    val_out, ret_out, anc_out, mom_out,
    near, far, gv, go, w, a, m, gn, normed, pick_ref, padded, parts, stat_send, stat_recv,
    inv_ref, dot_ref, grad, og, anc, mom, vals, vsend, vrecv, zsend, zrecv, vout,
    b_scat, b_slot, b_cross, b_turn,
    scat_0, scat_1, scat_2, scat_3, scat_4, scat_5, scat_6, scat_7, slot,
    cross_0, cross_1, cross_2, cross_3, cross_4, cross_5, cross_6, cross_7,
    turn, home, sel_p, rank_p, sel_f, rank_f, crosses, st_other, st_out,
    st_ss, st_rs, load_sem, fwd_send, fwd_recv, stat_sem, core_sem, z_sem, out_sem,
    bs_sem, bx_sem, bt_sem, s_ss, s_rs, x_ss, x_rs, t_ss, t_rs,
):
    rep = lax.axis_index("rep")
    sec = lax.axis_index("section")
    tp = lax.axis_index("tp")
    core = lax.rem(tp, 2)
    zlo = tp // 2
    other = 1 - rep
    after = lax.rem(sec + 1, SECTIONS)
    before = lax.rem(sec + SECTIONS - 1, SECTIONS)
    sibling = 2 * zlo + 1 - core

    scat = (scat_0, scat_1, scat_2, scat_3, scat_4, scat_5, scat_6, scat_7)
    cross = (cross_0, cross_1, cross_2, cross_3, cross_4, cross_5, cross_6, cross_7)

    def column(d):
        return lax.rem(sec + d, SECTIONS)

    loads = [
        pltpu.make_async_copy(src, dst, load_sem.at[i])
        for i, (src, dst) in enumerate(
            [(gv_hbm, gv), (w_hbm, w), (go_hbm, go), (a_hbm, a), (m_hbm, m), (flags_hbm, crosses)]
        )
    ]
    for load in loads:
        load.start()

    barrier = pltpu.get_barrier_semaphore()
    peers = [(other, sec, tp), (other, after, tp), (other, before, tp)]
    peers += [(rep, column(d), tp) for d in range(1, SECTIONS)]
    peers += [(rep, sec, lax.rem(tp + d, 8)) for d in range(1, 8)]
    with jax.named_scope("entry"):
        for peer in peers:
            pl.semaphore_signal(barrier, inc=1, device_id=peer, device_id_type=MESH)
        pl.semaphore_wait(barrier, len(peers))

    fwd = [
        remote(up_hbm, far, fwd_send.at[0], fwd_recv.at[0], (other, after, tp)),
        remote(up_hbm, near, fwd_send.at[1], fwd_recv.at[1], (rep, after, tp)),
    ]
    for copy in fwd:
        copy.start()

    loads[5].wait()
    for first, sel, rank, count in ((0, sel_p, rank_p, kp), (SECTIONS, sel_f, rank_f, kf)):
        flags = [crosses[first + i] for i in range(SECTIONS)]
        seen = jnp.int32(0)
        chosen = [jnp.int32(0)] * count
        for i in range(SECTIONS):
            rank[i] = jnp.minimum(seen, count - 1)
            chosen = [
                jnp.where((flags[i] != 0) & (seen == k), i, chosen[k]) if k <= i else chosen[k]
                for k in range(count)
            ]
            seen = seen + flags[i]
        for k in range(count):
            sel[k] = chosen[k]

    for load in loads[:3]:
        load.wait()

    def grad_normed(j, _):
        cols = pl.ds(pl.multiple_of(j * WIDE, WIDE), WIDE)
        product = lax.dot_general(
            gv[...], w[cols, :], (((1,), (1,)), ((), ())), preferred_element_type=F32
        )
        gn[:, cols] = product * scale + go[:, cols].astype(F32)
        return _

    with jax.named_scope("grad_normed"):
        lax.fori_loop(0, W // WIDE, grad_normed, 0)
    parts[...] = jnp.zeros_like(parts)

    with jax.named_scope("arrive"):
        for copy in fwd:
            copy.wait()

    take_near = crosses[SECTIONS + before] == 0

    def statistics(j, _):
        cols = lanes(j)
        x = jnp.where(take_near, near[:, cols].astype(F32), far[:, cols].astype(F32))
        near[:, cols] = x.astype(BF16)
        parts[0, 0:TOK, :] += x * x
        parts[1, 0:TOK, :] += x * gain_ref[:, cols] * gn[:, cols]
        return _

    with jax.named_scope("statistics"):
        lax.fori_loop(0, BLOCKS, statistics, 0)

        ones = jnp.full((8, LANE), 1.0, F32)
        row_id = lax.broadcasted_iota(jnp.int32, (8, LANE), 0)
        packed = jnp.zeros((8, LANE), F32)
        for i in range(2):
            row = lax.dot_general(
                ones, parts[i], (((1,), (1,)), ((), ())),
                preferred_element_type=F32, precision=lax.Precision.HIGHEST,
            )
            for k in range(3):
                packed = jnp.where(row_id == 3 * i + k, row[:, k * LANE : (k + 1) * LANE], packed)
        stat_send[...] = packed
        stat_recv[0] = packed
    for d in range(1, 8):
        remote(
            stat_send, stat_recv.at[d], stat_sem.at[0], stat_sem.at[1],
            (rep, sec, lax.rem(tp + d, 8)),
        ).start()
    stat_all = remote(
        stat_recv.at[pl.ds(1, 7)], stat_recv.at[pl.ds(1, 7)],
        stat_sem.at[0], stat_sem.at[1], (other, sec, tp),
    )
    with jax.named_scope("stat_wait"):
        stat_all.wait()

    def b_piece(j):
        return (pl.ds(pl.multiple_of(STRAIGHT + (j // 8) * HALF, 16), HALF), lanes(lax.rem(j, 8)))

    def b_scatter(d):
        q = column(d)
        return remote(
            grad.at[b_piece(q)], b_scat.at[sec], bs_sem.at[0], bs_sem.at[1], (rep, q, tp)
        )

    def b_gather(d):
        q = column(d)
        return remote(
            b_turn.at[q], ret_out.at[b_piece(sec)], bt_sem.at[0], bt_sem.at[1], (rep, q, tp)
        )

    def every(buffer, send_sem, recv_sem):
        ref = buffer.at[pl.ds(0, SECTIONS - 1)]
        return remote(ref, ref, send_sem, recv_sem, (other, sec, tp))

    b_scatter_all = every(b_scat, bs_sem.at[0], bs_sem.at[1])
    b_gather_all = every(b_turn, bt_sem.at[0], bt_sem.at[1])
    scatter_all = [every(scat[h], s_ss.at[h], s_rs.at[h]) for h in range(PHASES)]
    gather_all = [every(home.at[h], t_ss.at[h], t_rs.at[h]) for h in range(PHASES)]
    b_swap = remote(b_slot, b_cross, bx_sem.at[0], bx_sem.at[1], (other, sec, tp))

    def strip(h):
        return (h // 2, slice(None), pl.ds(WIDTH * (h % 2), WIDTH))

    def scatter(h, d):
        q = column(d)
        return remote(og.at[(q, *strip(h))], scat[h].at[sec], s_ss.at[h], s_rs.at[h], (rep, q, tp))

    def swap(h):
        return remote(slot.at[h], cross[h], x_ss.at[h], x_rs.at[h], (other, sec, tp))

    def gather(h, d):
        q = column(d)
        return remote(turn.at[h, q], home.at[h, sec], t_ss.at[h], t_rs.at[h], (rep, q, tp))

    def each(first, last, body):
        def step(i, _):
            body(i)
            return _

        lax.fori_loop(first, last, step, 0)

    with jax.named_scope("input_gradient"):
        total = jnp.sum(stat_recv[...], axis=0)
        for i in range(2):
            for k in range(3):
                spread = lax.dot_general(
                    total, jnp.where(row_id == 3 * i + k, 1.0, 0.0), (((0,), (0,)), ((), ())),
                    preferred_element_type=F32, precision=lax.Precision.HIGHEST,
                )
                parts[i, k * LANE : (k + 1) * LANE, :] = spread
        inv = lax.rsqrt(parts[0, 0:TOK, :] / D + eps)
        inv_ref[...] = inv
        dot_ref[...] = inv * inv * inv * parts[1, 0:TOK, :] / D

        def input_gradient(j):
            cols = lanes(j)
            x = near[:, cols].astype(F32)
            gain = gain_ref[:, cols]
            inv = inv_ref[...]
            grad[:, cols] = (inv * gain * gn[:, cols] - x * dot_ref[...]).astype(BF16)
            normed[:, cols] = (x * inv * gain).astype(BF16)

        each(0, BLOCKS, input_gradient)
    first_rows = pl.ds(0, STRAIGHT)
    st_swap = remote(grad.at[first_rows], st_other, st_ss.at[0], st_rs.at[0], (other, sec, tp))
    st_hop = remote(st_out, ret_out.at[first_rows], st_ss.at[1], st_rs.at[1], (rep, before, tp))
    st_swap.start()
    each(1, SECTIONS, lambda d: b_scatter(d).start())
    mine = b_piece(sec)
    b_scat[sec] = grad[mine]

    with jax.named_scope("values"):
        out_row = lax.broadcasted_iota(jnp.int32, (PAD, TOK), 0)
        in_row = lax.broadcasted_iota(jnp.int32, (PAD, TOK), 1)
        place = lax.rem(out_row, ROWS)
        pick = jnp.where((in_row == (out_row // ROWS) * OWN + place) & (place < OWN), 1.0, 0.0)
        pick_ref[...] = pick.astype(BF16)

        def pad_rows(j):
            cols = pl.ds(pl.multiple_of(j * WIDE, WIDE), WIDE)
            padded[:, cols] = jnp.dot(
                pick_ref[...], normed[:, cols], preferred_element_type=F32
            ).astype(BF16)

        each(0, W // WIDE, pad_rows)

        def partial_values(j):
            cols = pl.ds(pl.multiple_of(j * WIDE, WIDE), WIDE)
            product = jnp.dot(padded[...], w[:, cols], preferred_element_type=F32) * scale
            vals[:, :, cols] = product.reshape(8, ROWS, WIDE)

        each(0, W // WIDE, partial_values)
        for z in range(4):
            vsend[z] = vals[2 * z + 1 - core].astype(BF16)
        core_copy = remote(vsend, vrecv, core_sem.at[0], core_sem.at[1], (rep, sec, sibling))
        core_copy.start()

    loads[3].wait()
    loads[4].wait()

    def outer_gradient(i):
        c = lax.rem(sec // 2 + i, BLOCKS)
        rows = lanes(c)
        weight_grad = lax.dot_general(
            normed[:, rows], gv[...], (((0,), (0,)), ((), ())), preferred_element_type=F32
        ) * scale
        local_new = w[rows, :].astype(F32) - inner_rate * weight_grad
        anchor = a[pl.ds(2 * c, 2)].reshape(LANE, W).astype(F32)
        og[pl.ds(2 * c, 2)] = (anchor - local_new).astype(BF16).reshape(2, STRIPS, 16, W)
        for e in range(2):
            d = lax.rem(2 * c + e - sec + SECTIONS, SECTIONS)

            @pl.when(d != 0)
            def _():
                scatter(0, d).start()

    with jax.named_scope("outer_gradient"):
        each(0, BLOCKS, outer_gradient)
    for h in range(PHASES):
        scat[h][sec] = og[(sec, *strip(h))]
    with jax.named_scope("values_send"):
        core_copy.wait()
        for d in range(1, 4):
            z = lax.rem(zlo + d, 4)
            zsend[d] = (vals[2 * z + core] + vrecv[z].astype(F32)).astype(BF16)
            remote(
                zsend.at[d], zrecv.at[d], z_sem.at[0], z_sem.at[1], (rep, sec, 2 * z + core)
            ).start()
    z_all = remote(
        zrecv.at[pl.ds(1, 3)], zrecv.at[pl.ds(1, 3)], z_sem.at[0], z_sem.at[1], (other, sec, tp)
    )
    each(1, SECTIONS, lambda d: scatter(1, d).start())

    def cross_back():
        with jax.named_scope("back_scatter_wait"):
            b_scatter_all.wait_recv()

        def fill(k):
            b_slot[k] = b_scat[lax.rem(sel_f[k] + 1, SECTIONS)]

        each(0, kf, fill)
        b_swap.start()

    def turn_back():
        def fill(i):
            flipped = crosses[SECTIONS + i] != 0
            crossed = b_cross[rank_f[i]].astype(F32)
            stayed = b_scat[lax.rem(i + 1, SECTIONS)].astype(F32)
            b_turn[i] = jnp.where(flipped, crossed, stayed).astype(BF16)

        each(0, SECTIONS, fill)
        each(1, SECTIONS, lambda d: b_gather(d).start())
        b_home.start()

    b_home = pltpu.make_async_copy(b_turn.at[sec], ret_out.at[mine], out_sem.at[2 * PHASES + 1])

    def cross_out(h):
        with jax.named_scope("scatter_wait"):
            scatter_all[h].wait_recv()

        def fill(k):
            slot[h, k] = scat[h][sel_p[k]]

        each(0, kp, fill)
        swap(h).start()

    def crossed_out(h):
        with jax.named_scope("cross_wait"):
            swap(h).wait_recv()

    def turn_out(h):
        def fill(i):
            turn[h, i] = cross[h][rank_p[i]]

        each(0, SECTIONS, fill)
        each(1, SECTIONS, lambda d: gather(h, d).start())
        home[h, sec] = turn[h, sec]

    paired = crosses[sec] != 0

    def out_copies(h):
        part = (slice(None), *strip(h))
        return (
            pltpu.make_async_copy(anc.at[part], anc_out.at[part], out_sem.at[h]),
            pltpu.make_async_copy(mom.at[part], mom_out.at[part], out_sem.at[h + PHASES]),
        )

    def outer_step(h):
        with jax.named_scope("gather_wait"):
            gather_all[h].wait_recv()

        def step(j):
            part = (j, *strip(h))
            own = og[part].astype(F32)
            chosen = jnp.where(paired, home[h, j].astype(F32), own)
            mean_grad = 0.5 * (own + chosen)
            momentum_next = keep_rate * m[part].astype(F32) + mean_grad
            anc[part] = (
                a[part].astype(F32) - outer_rate * (mean_grad + keep_rate * momentum_next)
            ).astype(BF16)
            mom[part] = momentum_next.astype(BF16)

        with jax.named_scope("outer_step"):
            each(0, SECTIONS, step)
        for copy in out_copies(h):
            copy.start()

    def send_out(h):
        if h < PHASES:
            each(1, SECTIONS, lambda d: scatter(h, d).start())

    def pass_on():
        with jax.named_scope("straight_wait"):
            st_swap.wait_recv()
        stays = crosses[SECTIONS + before] == 0

        def pick(j):
            cols = lanes(j)
            x = jnp.where(stays, grad[0:STRAIGHT, cols].astype(F32), st_other[:, cols].astype(F32))
            st_out[:, cols] = x.astype(BF16)

        each(0, BLOCKS, pick)
        st_hop.start()

    cross_back()
    send_out(2)
    cross_out(0)
    send_out(3)
    cross_out(1)
    send_out(4)
    send_out(5)
    pass_on()
    for h in range(2, 6):
        cross_out(h)
        send_out(h + 4)
    with jax.named_scope("back_cross_wait"):
        b_swap.wait_recv()
    turn_back()
    for h in range(PHASES):
        crossed_out(h)
        if h + 6 < PHASES:
            cross_out(h + 6)
        turn_out(h)
        send_out(h + 6+4)
        if h >= 2:
            outer_step(h - 2)

    total = vals[2 * zlo + core] + vrecv[zlo].astype(F32)
    with jax.named_scope("values_wait"):
        z_all.wait()
    for d in range(1, 4):
        total = total + zrecv[d].astype(F32)
    vout[...] = total.astype(BF16)
    val_copy = pltpu.make_async_copy(vout, val_out, out_sem.at[2 * PHASES])
    val_copy.start()


    outer_step(PHASES - 2)
    with jax.named_scope("back_gather_wait"):
        b_gather_all.wait_recv()
    outer_step(PHASES - 1)

    with jax.named_scope("finish"):
        b_swap.wait_send()
        for h in range(PHASES):
            swap(h).wait_send()

        for copy in [b_scatter_all, b_gather_all] + scatter_all + gather_all:
            copy.wait_send()
        b_home.wait()
        st_swap.wait_send()
        st_hop.wait()
        val_copy.wait()
        for h in range(PHASES):
            for copy in out_copies(h):
                copy.wait()


def finish_kernel(val, ret, anc, mom, val_out, ret_out, anc_out, mom_out, *scratch):
    into, out = scratch[-2:]
    parts = []
    for src, held, dst, cuts in zip(
        (anc, mom, ret), scratch[:3], (anc_out, mom_out, ret_out), (4, 4, 2)
    ):
        size = held.shape[0] // cuts
        for i in range(cuts):
            rows = pl.ds(i * size, size)
            n = len(parts)
            parts.append((
                pltpu.make_async_copy(src.at[rows], held.at[rows], into.at[n]),
                pltpu.make_async_copy(held.at[rows], dst.at[rows], out.at[n]),
            ))
    for first, _ in parts:
        first.start()
    val_out[...] = val[0:OWN, :]
    for first, second in parts:
        first.wait()
        second.start()
    for _, second in parts:
        second.wait()


def layer(kp, kf, collective_id, *args):
    any_spec = pl.BlockSpec(memory_space=pl.ANY)
    vmem_spec = pl.BlockSpec(memory_space=pltpu.VMEM)
    dma = pltpu.SemaphoreType.DMA
    tokens = pltpu.VMEM((TOK, W), BF16)
    square = pltpu.VMEM((W, W), BF16)
    cut = pltpu.VMEM((SECTIONS, STRIPS, 16, W), BF16)
    table = pltpu.SMEM((SECTIONS,), jnp.int32)

    def pieces(count):
        return pltpu.VMEM((count, HALF, LANE), BF16)

    def rows(count):
        return pltpu.VMEM((count, 16, WIDTH), BF16)

    def slots(count):
        return pltpu.VMEM((PHASES, count, 16, WIDTH), BF16)

    return pl.pallas_call(
        functools.partial(kernel, kp, kf),
        out_shape=(
            jax.ShapeDtypeStruct((ROWS, W), BF16),
            jax.ShapeDtypeStruct((TOK, W), BF16),
            jax.ShapeDtypeStruct((SECTIONS, STRIPS, 16, W), BF16),
            jax.ShapeDtypeStruct((SECTIONS, STRIPS, 16, W), BF16),
        ),
        in_specs=[any_spec, vmem_spec] + [any_spec] * 6,
        out_specs=(any_spec,) * 4,
        scratch_shapes=[
            tokens, tokens, tokens, tokens, square, cut, cut,
            pltpu.VMEM((TOK, W), F32),
            tokens,
            pltpu.VMEM((PAD, TOK), BF16),
            pltpu.VMEM((PAD, W), BF16),
            pltpu.VMEM((2, PAD, LANE), F32),
            pltpu.VMEM((8, LANE), F32),
            pltpu.VMEM((8, 8, LANE), F32),
            pltpu.VMEM((TOK, LANE), F32),
            pltpu.VMEM((TOK, LANE), F32),
            tokens,
            cut, cut, cut,
            pltpu.VMEM((8, ROWS, W), F32),
            pltpu.VMEM((4, ROWS, W), BF16),
            pltpu.VMEM((4, ROWS, W), BF16),
            pltpu.VMEM((4, ROWS, W), BF16),
            pltpu.VMEM((4, ROWS, W), BF16),
            pltpu.VMEM((ROWS, W), BF16),
            pieces(SECTIONS), pieces(kf), pieces(kf), pieces(SECTIONS),
            *[rows(SECTIONS)] * PHASES, slots(kp), *[rows(kp)] * PHASES, slots(SECTIONS), slots(SECTIONS),
            table, table, table, table, pltpu.SMEM((2 * SECTIONS,), jnp.int32),
            *[pltpu.VMEM((STRAIGHT, W), BF16)] * 2,
            dma((2,)), dma((2,)),
            dma((6,)), dma((2,)), dma((2,)), dma((2,)), dma((2,)), dma((2,)), dma((2 * PHASES + 2,)),
            dma((2,)), dma((2,)), dma((2,)),
            dma((PHASES,)), dma((PHASES,)), dma((PHASES,)), dma((PHASES,)), dma((PHASES,)), dma((PHASES,)),
        ],
        compiler_params=pltpu.CompilerParams(
            collective_id=collective_id, has_side_effects=True, vmem_limit_bytes=56 * 2**20
        ),
        cost_estimate=pl.CostEstimate(
            flops=6 * TOK * W * W, bytes_accessed=13 * 2**20, transcendentals=TOK * LANE
        ),
        name="layer",
    )(*args)


ROOM = ((8, 11), (11, 12), (SECTIONS, SECTIONS))


def on_device(
    upstream, norm_gain, grad_values, grad_other, local_weights, anchor, momentum,
    section_routes, pairing,
):
    cut = (SECTIONS, STRIPS, 16, W)
    flags = jnp.concatenate([pairing[:, 0], section_routes[:, 0]])
    args = (
        upstream[0, 0], norm_gain[None, :], grad_values[0, 0], grad_other[0, 0],
        local_weights[0, 0], anchor.reshape(cut), momentum.reshape(cut), flags,
    )
    crossing = jnp.sum(flags.reshape(2, SECTIONS), axis=1)
    branch = jnp.int32(0)
    for kp, kf in ROOM[:-1]:
        branch += ((crossing[0] > kp) | (crossing[1] > kf)).astype(jnp.int32)
    outs = lax.switch(
        branch, [functools.partial(layer, kp, kf, i) for i, (kp, kf) in enumerate(ROOM)], *args
    )
    any_spec = pl.BlockSpec(memory_space=pl.ANY)
    vmem_spec = pl.BlockSpec(memory_space=pltpu.VMEM)
    values, returned, anchor_new, momentum_new = pl.pallas_call(
        finish_kernel,
        out_shape=(
            jax.ShapeDtypeStruct((OWN, W), BF16),
            jax.ShapeDtypeStruct((TOK, W), BF16),
            jax.ShapeDtypeStruct(cut, BF16),
            jax.ShapeDtypeStruct(cut, BF16),
        ),
        in_specs=[vmem_spec] + [any_spec] * 3,
        out_specs=(vmem_spec,) + (any_spec,) * 3,
        scratch_shapes=[
            pltpu.VMEM(cut, BF16), pltpu.VMEM(cut, BF16), pltpu.VMEM((TOK, W), BF16),
            pltpu.SemaphoreType.DMA((10,)), pltpu.SemaphoreType.DMA((10,)),
        ],
        compiler_params=pltpu.CompilerParams(vmem_limit_bytes=32 * 2**20),
        name="finish",
    )(*outs)
    return (
        values[None, None],
        returned[None, None],
        anchor_new.reshape(1, 1, W, W),
        momentum_new.reshape(1, 1, W, W),
    )


def solution(mesh):
    return jax.shard_map(
        on_device,
        mesh=mesh,
        in_specs=(
            P("rep", "section", None, "tp"),
            P("tp"),
            P("rep", "section", None, None),
            P("rep", "section", None, "tp"),
            P("rep", "section", "tp", None),
            P("rep", "section", "tp", None),
            P("rep", "section", "tp", None),
            P(),
            P(),
        ),
        out_specs=(
            P("rep", "section", "tp", None),
            P("rep", "section", None, "tp"),
            P("rep", "section", "tp", None),
            P("rep", "section", "tp", None),
        ),
        check_vma=False,
    )
```

```python
import functools

import jax
import jax.numpy as jnp
from jax import lax
from jax.experimental import pallas as pl
from jax.experimental.pallas import tpu as pltpu
from jax.sharding import PartitionSpec as P

MESH = pl.DeviceIdType.MESH
F32 = jnp.float32
BF16 = jnp.bfloat16

D = 8192
eps = 1e-05
inner_rate = 1.0
outer_rate = 0.7
keep_rate = 0.9
scale = D ** (-0.5)

TOK = 352
PAD = 384
OWN = 44
ROWS = 48
W = 1024
LANE = 128
BLOCKS = W // LANE
SECTIONS = 16
STRIPS = 4
PHASES = 8
WIDTH = W // 2
STRAIGHT = 128
HALF = (TOK - STRAIGHT) // 2
WIDE = 256


def remote(src, dst, send_sem, recv_sem, device):
    return pltpu.make_async_remote_copy(
        src_ref=src, dst_ref=dst, send_sem=send_sem, recv_sem=recv_sem,
        device_id=device, device_id_type=MESH,
    )


def lanes(j):
    return pl.ds(pl.multiple_of(j * LANE, LANE), LANE)


def kernel(
    kp, kf,
    up_hbm, gain_ref, gv_hbm, go_hbm, w_hbm, a_hbm, m_hbm, flags_hbm,
    val_out, ret_out, anc_out, mom_out,
    near, far, gv, go, w, a, m, gn, normed, pick_ref, padded, parts, stat_send, stat_recv,
    inv_ref, dot_ref, grad, og, anc, mom, vals, vsend, vrecv, zsend, zrecv, vout,
    b_scat, b_slot, b_cross, b_turn,
    scat_0, scat_1, scat_2, scat_3, scat_4, scat_5, scat_6, scat_7, slot,
    cross_0, cross_1, cross_2, cross_3, cross_4, cross_5, cross_6, cross_7,
    turn, home, sel_p, rank_p, sel_f, rank_f, crosses, st_other, st_out,
    st_ss, st_rs, load_sem, fwd_send, fwd_recv, stat_sem, core_sem, z_sem, out_sem,
    bs_sem, bx_sem, bt_sem, s_ss, s_rs, x_ss, x_rs, t_ss, t_rs,
):
    rep = lax.axis_index("rep")
    sec = lax.axis_index("section")
    tp = lax.axis_index("tp")
    core = lax.rem(tp, 2)
    zlo = tp // 2
    other = 1 - rep
    after = lax.rem(sec + 1, SECTIONS)
    before = lax.rem(sec + SECTIONS - 1, SECTIONS)
    sibling = 2 * zlo + 1 - core

    scat = (scat_0, scat_1, scat_2, scat_3, scat_4, scat_5, scat_6, scat_7)
    cross = (cross_0, cross_1, cross_2, cross_3, cross_4, cross_5, cross_6, cross_7)

    def column(d):
        return lax.rem(sec + d, SECTIONS)

    loads = [
        pltpu.make_async_copy(src, dst, load_sem.at[i])
        for i, (src, dst) in enumerate(
            [(gv_hbm, gv), (w_hbm, w), (go_hbm, go), (a_hbm, a), (m_hbm, m), (flags_hbm, crosses)]
        )
    ]
    for load in loads:
        load.start()

    barrier = pltpu.get_barrier_semaphore()
    peers = [(other, sec, tp), (other, after, tp), (other, before, tp)]
    peers += [(rep, column(d), tp) for d in range(1, SECTIONS)]
    peers += [(rep, sec, lax.rem(tp + d, 8)) for d in range(1, 8)]
    with jax.named_scope("entry"):
        for peer in peers:
            pl.semaphore_signal(barrier, inc=1, device_id=peer, device_id_type=MESH)
        pl.semaphore_wait(barrier, len(peers))

    fwd = [
        remote(up_hbm, far, fwd_send.at[0], fwd_recv.at[0], (other, after, tp)),
        remote(up_hbm, near, fwd_send.at[1], fwd_recv.at[1], (rep, after, tp)),
    ]
    for copy in fwd:
        copy.start()

    loads[5].wait()
    for first, sel, rank, count in ((0, sel_p, rank_p, kp), (SECTIONS, sel_f, rank_f, kf)):
        flags = [crosses[first + i] for i in range(SECTIONS)]
        seen = jnp.int32(0)
        chosen = [jnp.int32(0)] * count
        for i in range(SECTIONS):
            rank[i] = jnp.minimum(seen, count - 1)
            chosen = [
                jnp.where((flags[i] != 0) & (seen == k), i, chosen[k]) if k <= i else chosen[k]
                for k in range(count)
            ]
            seen = seen + flags[i]
        for k in range(count):
            sel[k] = chosen[k]

    for load in loads[:3]:
        load.wait()

    def grad_normed(j, _):
        cols = pl.ds(pl.multiple_of(j * WIDE, WIDE), WIDE)
        product = lax.dot_general(
            gv[...], w[cols, :], (((1,), (1,)), ((), ())), preferred_element_type=F32
        )
        gn[:, cols] = product * scale + go[:, cols].astype(F32)
        return _

    with jax.named_scope("grad_normed"):
        lax.fori_loop(0, W // WIDE, grad_normed, 0)
    parts[...] = jnp.zeros_like(parts)

    with jax.named_scope("arrive"):
        for copy in fwd:
            copy.wait()

    take_near = crosses[SECTIONS + before] == 0

    def statistics(j, _):
        cols = lanes(j)
        x = jnp.where(take_near, near[:, cols].astype(F32), far[:, cols].astype(F32))
        near[:, cols] = x.astype(BF16)
        parts[0, 0:TOK, :] += x * x
        parts[1, 0:TOK, :] += x * gain_ref[:, cols] * gn[:, cols]
        return _

    with jax.named_scope("statistics"):
        lax.fori_loop(0, BLOCKS, statistics, 0)

        ones = jnp.full((8, LANE), 1.0, F32)
        row_id = lax.broadcasted_iota(jnp.int32, (8, LANE), 0)
        packed = jnp.zeros((8, LANE), F32)
        for i in range(2):
            row = lax.dot_general(
                ones, parts[i], (((1,), (1,)), ((), ())),
                preferred_element_type=F32, precision=lax.Precision.HIGHEST,
            )
            for k in range(3):
                packed = jnp.where(row_id == 3 * i + k, row[:, k * LANE : (k + 1) * LANE], packed)
        stat_send[...] = packed
        stat_recv[0] = packed
    for d in range(1, 8):
        remote(
            stat_send, stat_recv.at[d], stat_sem.at[0], stat_sem.at[1],
            (rep, sec, lax.rem(tp + d, 8)),
        ).start()
    stat_all = remote(
        stat_recv.at[pl.ds(1, 7)], stat_recv.at[pl.ds(1, 7)],
        stat_sem.at[0], stat_sem.at[1], (other, sec, tp),
    )
    with jax.named_scope("stat_wait"):
        stat_all.wait()

    def b_piece(j):
        return (pl.ds(pl.multiple_of(STRAIGHT + (j // 8) * HALF, 16), HALF), lanes(lax.rem(j, 8)))

    def b_scatter(d):
        q = column(d)
        return remote(
            grad.at[b_piece(q)], b_scat.at[sec], bs_sem.at[0], bs_sem.at[1], (rep, q, tp)
        )

    def b_gather(d):
        q = column(d)
        return remote(
            b_turn.at[q], ret_out.at[b_piece(sec)], bt_sem.at[0], bt_sem.at[1], (rep, q, tp)
        )

    def every(buffer, send_sem, recv_sem):
        ref = buffer.at[pl.ds(0, SECTIONS - 1)]
        return remote(ref, ref, send_sem, recv_sem, (other, sec, tp))

    b_scatter_all = every(b_scat, bs_sem.at[0], bs_sem.at[1])
    b_gather_all = every(b_turn, bt_sem.at[0], bt_sem.at[1])
    scatter_all = [every(scat[h], s_ss.at[h], s_rs.at[h]) for h in range(PHASES)]
    gather_all = [every(home.at[h], t_ss.at[h], t_rs.at[h]) for h in range(PHASES)]
    b_swap = remote(b_slot, b_cross, bx_sem.at[0], bx_sem.at[1], (other, sec, tp))

    def strip(h):
        return (h // 2, slice(None), pl.ds(WIDTH * (h % 2), WIDTH))

    def scatter(h, d):
        q = column(d)
        return remote(og.at[(q, *strip(h))], scat[h].at[sec], s_ss.at[h], s_rs.at[h], (rep, q, tp))

    def swap(h):
        return remote(slot.at[h], cross[h], x_ss.at[h], x_rs.at[h], (other, sec, tp))

    def gather(h, d):
        q = column(d)
        return remote(turn.at[h, q], home.at[h, sec], t_ss.at[h], t_rs.at[h], (rep, q, tp))

    def each(first, last, body):
        def step(i, _):
            body(i)
            return _

        lax.fori_loop(first, last, step, 0)

    with jax.named_scope("input_gradient"):
        total = jnp.sum(stat_recv[...], axis=0)
        for i in range(2):
            for k in range(3):
                spread = lax.dot_general(
                    total, jnp.where(row_id == 3 * i + k, 1.0, 0.0), (((0,), (0,)), ((), ())),
                    preferred_element_type=F32, precision=lax.Precision.HIGHEST,
                )
                parts[i, k * LANE : (k + 1) * LANE, :] = spread
        inv = lax.rsqrt(parts[0, 0:TOK, :] / D + eps)
        inv_ref[...] = inv
        dot_ref[...] = inv * inv * inv * parts[1, 0:TOK, :] / D

        def input_gradient(j):
            cols = lanes(j)
            x = near[:, cols].astype(F32)
            gain = gain_ref[:, cols]
            inv = inv_ref[...]
            grad[:, cols] = (inv * gain * gn[:, cols] - x * dot_ref[...]).astype(BF16)
            normed[:, cols] = (x * inv * gain).astype(BF16)

        each(0, BLOCKS, input_gradient)
    first_rows = pl.ds(0, STRAIGHT)
    st_swap = remote(grad.at[first_rows], st_other, st_ss.at[0], st_rs.at[0], (other, sec, tp))
    st_hop = remote(st_out, ret_out.at[first_rows], st_ss.at[1], st_rs.at[1], (rep, before, tp))
    st_swap.start()
    each(1, SECTIONS, lambda d: b_scatter(d).start())
    mine = b_piece(sec)
    b_scat[sec] = grad[mine]

    with jax.named_scope("values"):
        out_row = lax.broadcasted_iota(jnp.int32, (PAD, TOK), 0)
        in_row = lax.broadcasted_iota(jnp.int32, (PAD, TOK), 1)
        place = lax.rem(out_row, ROWS)
        pick = jnp.where((in_row == (out_row // ROWS) * OWN + place) & (place < OWN), 1.0, 0.0)
        pick_ref[...] = pick.astype(BF16)

        def pad_rows(j):
            cols = pl.ds(pl.multiple_of(j * WIDE, WIDE), WIDE)
            padded[:, cols] = jnp.dot(
                pick_ref[...], normed[:, cols], preferred_element_type=F32
            ).astype(BF16)

        each(0, W // WIDE, pad_rows)

        def partial_values(j):
            cols = pl.ds(pl.multiple_of(j * WIDE, WIDE), WIDE)
            product = jnp.dot(padded[...], w[:, cols], preferred_element_type=F32) * scale
            vals[:, :, cols] = product.reshape(8, ROWS, WIDE)

        each(0, W // WIDE, partial_values)
        for z in range(4):
            vsend[z] = vals[2 * z + 1 - core].astype(BF16)
        core_copy = remote(vsend, vrecv, core_sem.at[0], core_sem.at[1], (rep, sec, sibling))
        core_copy.start()

    loads[3].wait()
    loads[4].wait()

    def outer_gradient(i):
        c = lax.rem(sec // 2 + i, BLOCKS)
        rows = lanes(c)
        weight_grad = lax.dot_general(
            normed[:, rows], gv[...], (((0,), (0,)), ((), ())), preferred_element_type=F32
        ) * scale
        local_new = w[rows, :].astype(F32) - inner_rate * weight_grad
        anchor = a[pl.ds(2 * c, 2)].reshape(LANE, W).astype(F32)
        og[pl.ds(2 * c, 2)] = (anchor - local_new).astype(BF16).reshape(2, STRIPS, 16, W)
        for e in range(2):
            d = lax.rem(2 * c + e - sec + SECTIONS, SECTIONS)

            @pl.when(d != 0)
            def _():
                scatter(0, d).start()

    with jax.named_scope("outer_gradient"):
        each(0, BLOCKS, outer_gradient)
    for h in range(PHASES):
        scat[h][sec] = og[(sec, *strip(h))]
    with jax.named_scope("values_send"):
        core_copy.wait()
        for d in range(1, 4):
            z = lax.rem(zlo + d, 4)
            zsend[d] = (vals[2 * z + core] + vrecv[z].astype(F32)).astype(BF16)
            remote(
                zsend.at[d], zrecv.at[d], z_sem.at[0], z_sem.at[1], (rep, sec, 2 * z + core)
            ).start()
    z_all = remote(
        zrecv.at[pl.ds(1, 3)], zrecv.at[pl.ds(1, 3)], z_sem.at[0], z_sem.at[1], (other, sec, tp)
    )
    each(1, SECTIONS, lambda d: scatter(1, d).start())

    def cross_back():
        with jax.named_scope("back_scatter_wait"):
            b_scatter_all.wait_recv()

        def fill(k):
            b_slot[k] = b_scat[lax.rem(sel_f[k] + 1, SECTIONS)]

        each(0, kf, fill)
        b_swap.start()

    def turn_back():
        def fill(i):
            flipped = crosses[SECTIONS + i] != 0
            crossed = b_cross[rank_f[i]].astype(F32)
            stayed = b_scat[lax.rem(i + 1, SECTIONS)].astype(F32)
            b_turn[i] = jnp.where(flipped, crossed, stayed).astype(BF16)

        each(0, SECTIONS, fill)
        each(1, SECTIONS, lambda d: b_gather(d).start())
        b_home.start()

    b_home = pltpu.make_async_copy(b_turn.at[sec], ret_out.at[mine], out_sem.at[2 * PHASES + 1])

    def cross_out(h):
        with jax.named_scope("scatter_wait"):
            scatter_all[h].wait_recv()

        def fill(k):
            slot[h, k] = scat[h][sel_p[k]]

        each(0, kp, fill)
        swap(h).start()

    def crossed_out(h):
        with jax.named_scope("cross_wait"):
            swap(h).wait_recv()

    def turn_out(h):
        def fill(i):
            turn[h, i] = cross[h][rank_p[i]]

        each(0, SECTIONS, fill)
        each(1, SECTIONS, lambda d: gather(h, d).start())
        home[h, sec] = turn[h, sec]

    paired = crosses[sec] != 0

    def out_copies(h):
        part = (slice(None), *strip(h))
        return (
            pltpu.make_async_copy(anc.at[part], anc_out.at[part], out_sem.at[h]),
            pltpu.make_async_copy(mom.at[part], mom_out.at[part], out_sem.at[h + PHASES]),
        )

    def outer_step(h):
        with jax.named_scope("gather_wait"):
            gather_all[h].wait_recv()

        def step(j):
            part = (j, *strip(h))
            own = og[part].astype(F32)
            chosen = jnp.where(paired, home[h, j].astype(F32), own)
            mean_grad = 0.5 * (own + chosen)
            momentum_next = keep_rate * m[part].astype(F32) + mean_grad
            anc[part] = (
                a[part].astype(F32) - outer_rate * (mean_grad + keep_rate * momentum_next)
            ).astype(BF16)
            mom[part] = momentum_next.astype(BF16)

        with jax.named_scope("outer_step"):
            each(0, SECTIONS, step)
        for copy in out_copies(h):
            copy.start()

    def send_out(h):
        if h < PHASES:
            each(1, SECTIONS, lambda d: scatter(h, d).start())

    def pass_on():
        with jax.named_scope("straight_wait"):
            st_swap.wait_recv()
        stays = crosses[SECTIONS + before] == 0

        def pick(j):
            cols = lanes(j)
            x = jnp.where(stays, grad[0:STRAIGHT, cols].astype(F32), st_other[:, cols].astype(F32))
            st_out[:, cols] = x.astype(BF16)

        each(0, BLOCKS, pick)
        st_hop.start()

    cross_back()
    send_out(2)
    cross_out(0)
    send_out(3)
    cross_out(1)
    send_out(4)
    send_out(5)
    pass_on()
    for h in range(2, 6):
        cross_out(h)
        send_out(h + 4)
    with jax.named_scope("back_cross_wait"):
        b_swap.wait_recv()
    turn_back()
    for h in range(PHASES):
        crossed_out(h)
        if h + 6 < PHASES:
            cross_out(h + 6)
        turn_out(h)
        send_out(h + 6+4)
        if h >= 2:
            outer_step(h - 2)

    total = vals[2 * zlo + core] + vrecv[zlo].astype(F32)
    with jax.named_scope("values_wait"):
        z_all.wait()
    for d in range(1, 4):
        total = total + zrecv[d].astype(F32)
    vout[...] = total.astype(BF16)
    val_copy = pltpu.make_async_copy(vout, val_out, out_sem.at[2 * PHASES])
    val_copy.start()


    outer_step(PHASES - 2)
    with jax.named_scope("back_gather_wait"):
        b_gather_all.wait_recv()
    outer_step(PHASES - 1)

    with jax.named_scope("finish"):
        b_swap.wait_send()
        for h in range(PHASES):
            swap(h).wait_send()

        for copy in [b_scatter_all, b_gather_all] + scatter_all + gather_all:
            copy.wait_send()
        b_home.wait()
        st_swap.wait_send()
        st_hop.wait()
        val_copy.wait()
        for h in range(PHASES):
            for copy in out_copies(h):
                copy.wait()


def finish_kernel(val, ret, anc, mom, val_out, ret_out, anc_out, mom_out, *scratch):
    into, out = scratch[-2:]
    parts = []
    for src, held, dst, cuts in zip(
        (anc, mom, ret), scratch[:3], (anc_out, mom_out, ret_out), (4, 4, 2)
    ):
        size = held.shape[0] // cuts
        for i in range(cuts):
            rows = pl.ds(i * size, size)
            n = len(parts)
            parts.append((
                pltpu.make_async_copy(src.at[rows], held.at[rows], into.at[n]),
                pltpu.make_async_copy(held.at[rows], dst.at[rows], out.at[n]),
            ))
    for first, _ in parts:
        first.start()
    val_out[...] = val[0:OWN, :]
    for first, second in parts:
        first.wait()
        second.start()
    for _, second in parts:
        second.wait()


def layer(kp, kf, collective_id, *args):
    any_spec = pl.BlockSpec(memory_space=pl.ANY)
    vmem_spec = pl.BlockSpec(memory_space=pltpu.VMEM)
    dma = pltpu.SemaphoreType.DMA
    tokens = pltpu.VMEM((TOK, W), BF16)
    square = pltpu.VMEM((W, W), BF16)
    cut = pltpu.VMEM((SECTIONS, STRIPS, 16, W), BF16)
    table = pltpu.SMEM((SECTIONS,), jnp.int32)

    def pieces(count):
        return pltpu.VMEM((count, HALF, LANE), BF16)

    def rows(count):
        return pltpu.VMEM((count, 16, WIDTH), BF16)

    def slots(count):
        return pltpu.VMEM((PHASES, count, 16, WIDTH), BF16)

    return pl.pallas_call(
        functools.partial(kernel, kp, kf),
        out_shape=(
            jax.ShapeDtypeStruct((ROWS, W), BF16),
            jax.ShapeDtypeStruct((TOK, W), BF16),
            jax.ShapeDtypeStruct((SECTIONS, STRIPS, 16, W), BF16),
            jax.ShapeDtypeStruct((SECTIONS, STRIPS, 16, W), BF16),
        ),
        in_specs=[any_spec, vmem_spec] + [any_spec] * 6,
        out_specs=(any_spec,) * 4,
        scratch_shapes=[
            tokens, tokens, tokens, tokens, square, cut, cut,
            pltpu.VMEM((TOK, W), F32),
            tokens,
            pltpu.VMEM((PAD, TOK), BF16),
            pltpu.VMEM((PAD, W), BF16),
            pltpu.VMEM((2, PAD, LANE), F32),
            pltpu.VMEM((8, LANE), F32),
            pltpu.VMEM((8, 8, LANE), F32),
            pltpu.VMEM((TOK, LANE), F32),
            pltpu.VMEM((TOK, LANE), F32),
            tokens,
            cut, cut, cut,
            pltpu.VMEM((8, ROWS, W), F32),
            pltpu.VMEM((4, ROWS, W), BF16),
            pltpu.VMEM((4, ROWS, W), BF16),
            pltpu.VMEM((4, ROWS, W), BF16),
            pltpu.VMEM((4, ROWS, W), BF16),
            pltpu.VMEM((ROWS, W), BF16),
            pieces(SECTIONS), pieces(kf), pieces(kf), pieces(SECTIONS),
            *[rows(SECTIONS)] * PHASES, slots(kp), *[rows(kp)] * PHASES, slots(SECTIONS), slots(SECTIONS),
            table, table, table, table, pltpu.SMEM((2 * SECTIONS,), jnp.int32),
            *[pltpu.VMEM((STRAIGHT, W), BF16)] * 2,
            dma((2,)), dma((2,)),
            dma((6,)), dma((2,)), dma((2,)), dma((2,)), dma((2,)), dma((2,)), dma((2 * PHASES + 2,)),
            dma((2,)), dma((2,)), dma((2,)),
            dma((PHASES,)), dma((PHASES,)), dma((PHASES,)), dma((PHASES,)), dma((PHASES,)), dma((PHASES,)),
        ],
        compiler_params=pltpu.CompilerParams(
            collective_id=collective_id, has_side_effects=True, vmem_limit_bytes=56 * 2**20
        ),
        cost_estimate=pl.CostEstimate(
            flops=6 * TOK * W * W, bytes_accessed=13 * 2**20, transcendentals=TOK * LANE
        ),
        name="layer",
    )(*args)


ROOM = ((6, 10), (8, 9), (8, 11), (9, 11), (11, 12), (SECTIONS, SECTIONS))


def room_kernel(pairing, routes, flags, branch):
    counts = []
    for first, table in ((0, pairing), (SECTIONS, routes)):
        count = jnp.int32(0)
        for i in range(SECTIONS):
            flag = table[0, i]
            flags[first + i] = flag
            count = count + flag
        counts.append(count)
    chosen = jnp.int32(len(ROOM) - 1)
    for i, (kp, kf) in reversed(list(enumerate(ROOM[:-1]))):
        chosen = jnp.where((counts[0] <= kp) & (counts[1] <= kf), i, chosen)
    branch[0] = chosen


def on_device(
    upstream, norm_gain, grad_values, grad_other, local_weights, anchor, momentum,
    section_routes, pairing,
):
    cut = (SECTIONS, STRIPS, 16, W)
    smem_spec = pl.BlockSpec(memory_space=pltpu.SMEM)
    flags, branch = pl.pallas_call(
        room_kernel,
        out_shape=(
            jax.ShapeDtypeStruct((2 * SECTIONS,), jnp.int32), jax.ShapeDtypeStruct((1,), jnp.int32)
        ),
        in_specs=[smem_spec] * 2,
        out_specs=(smem_spec,) * 2,
        name="room",
    )(pairing.T, section_routes.T)
    args = (
        upstream[0, 0], norm_gain[None, :], grad_values[0, 0], grad_other[0, 0],
        local_weights[0, 0], anchor.reshape(cut), momentum.reshape(cut), flags,
    )
    outs = lax.switch(
        branch[0], [functools.partial(layer, kp, kf, i) for i, (kp, kf) in enumerate(ROOM)], *args
    )
    any_spec = pl.BlockSpec(memory_space=pl.ANY)
    vmem_spec = pl.BlockSpec(memory_space=pltpu.VMEM)
    values, returned, anchor_new, momentum_new = pl.pallas_call(
        finish_kernel,
        out_shape=(
            jax.ShapeDtypeStruct((OWN, W), BF16),
            jax.ShapeDtypeStruct((TOK, W), BF16),
            jax.ShapeDtypeStruct(cut, BF16),
            jax.ShapeDtypeStruct(cut, BF16),
        ),
        in_specs=[vmem_spec] + [any_spec] * 3,
        out_specs=(vmem_spec,) + (any_spec,) * 3,
        scratch_shapes=[
            pltpu.VMEM(cut, BF16), pltpu.VMEM(cut, BF16), pltpu.VMEM((TOK, W), BF16),
            pltpu.SemaphoreType.DMA((10,)), pltpu.SemaphoreType.DMA((10,)),
        ],
        compiler_params=pltpu.CompilerParams(vmem_limit_bytes=32 * 2**20),
        name="finish",
    )(*outs)
    return (
        values[None, None],
        returned[None, None],
        anchor_new.reshape(1, 1, W, W),
        momentum_new.reshape(1, 1, W, W),
    )


def solution(mesh):
    return jax.shard_map(
        on_device,
        mesh=mesh,
        in_specs=(
            P("rep", "section", None, "tp"),
            P("tp"),
            P("rep", "section", None, None),
            P("rep", "section", None, "tp"),
            P("rep", "section", "tp", None),
            P("rep", "section", "tp", None),
            P("rep", "section", "tp", None),
            P(),
            P(),
        ),
        out_specs=(
            P("rep", "section", "tp", None),
            P("rep", "section", None, "tp"),
            P("rep", "section", "tp", None),
            P("rep", "section", "tp", None),
        ),
        check_vma=False,
    )
```

```python
import functools

import jax
import jax.numpy as jnp
from jax import lax
from jax.experimental import pallas as pl
from jax.experimental.pallas import tpu as pltpu
from jax.sharding import PartitionSpec as P

MESH = pl.DeviceIdType.MESH
F32 = jnp.float32
BF16 = jnp.bfloat16

D = 8192
eps = 1e-05
inner_rate = 1.0
outer_rate = 0.7
keep_rate = 0.9
scale = D ** (-0.5)

TOK = 352
PAD = 384
OWN = 44
ROWS = 48
W = 1024
LANE = 128
BLOCKS = W // LANE
SECTIONS = 16
STRIPS = 4
PHASES = 8
WIDTH = W // 2
STRAIGHT = 96
HALF = (TOK - STRAIGHT) // 2
WIDE = 256


def remote(src, dst, send_sem, recv_sem, device):
    return pltpu.make_async_remote_copy(
        src_ref=src, dst_ref=dst, send_sem=send_sem, recv_sem=recv_sem,
        device_id=device, device_id_type=MESH,
    )


def lanes(j):
    return pl.ds(pl.multiple_of(j * LANE, LANE), LANE)


def kernel(
    kp, kf,
    up_hbm, gain_ref, gv_hbm, go_hbm, w_hbm, a_hbm, m_hbm, flags_hbm,
    val_out, ret_out, anc_out, mom_out,
    near, far, gv, go, w, a, m, gn, normed, pick_ref, padded, parts, stat_send, stat_recv,
    inv_ref, dot_ref, grad, og, anc, mom, vals, vsend, vrecv, zsend, zrecv, vout,
    b_scat, b_slot, b_cross, b_turn,
    scat_0, scat_1, scat_2, scat_3, scat_4, scat_5, scat_6, scat_7, slot,
    cross_0, cross_1, cross_2, cross_3, cross_4, cross_5, cross_6, cross_7,
    turn, home, sel_p, rank_p, sel_f, rank_f, crosses, st_other, st_out,
    st_ss, st_rs, load_sem, fwd_send, fwd_recv, stat_sem, core_sem, z_sem, out_sem,
    bs_sem, bx_sem, bt_sem, s_ss, s_rs, x_ss, x_rs, t_ss, t_rs,
):
    rep = lax.axis_index("rep")
    sec = lax.axis_index("section")
    tp = lax.axis_index("tp")
    core = lax.rem(tp, 2)
    zlo = tp // 2
    other = 1 - rep
    after = lax.rem(sec + 1, SECTIONS)
    before = lax.rem(sec + SECTIONS - 1, SECTIONS)
    sibling = 2 * zlo + 1 - core

    scat = (scat_0, scat_1, scat_2, scat_3, scat_4, scat_5, scat_6, scat_7)
    cross = (cross_0, cross_1, cross_2, cross_3, cross_4, cross_5, cross_6, cross_7)

    def column(d):
        return lax.rem(sec + d, SECTIONS)

    def each(first, last, body):
        def step(i, _):
            body(i)
            return _

        lax.fori_loop(first, last, step, 0)

    loads = [
        pltpu.make_async_copy(src, dst, load_sem.at[i])
        for i, (src, dst) in enumerate(
            [(gv_hbm, gv), (w_hbm, w), (go_hbm, go), (a_hbm, a), (m_hbm, m), (flags_hbm, crosses)]
        )
    ]
    for load in loads:
        load.start()

    barrier = pltpu.get_barrier_semaphore()
    peers = [(other, sec, tp), (other, after, tp), (other, before, tp)]
    peers += [(rep, column(d), tp) for d in range(1, SECTIONS)]
    peers += [(rep, sec, lax.rem(tp + d, 8)) for d in range(1, 8)]
    with jax.named_scope("entry"):
        for peer in peers:
            pl.semaphore_signal(barrier, inc=1, device_id=peer, device_id_type=MESH)
        pl.semaphore_wait(barrier, len(peers))

    parted = (pl.ds(0, TOK // 2), pl.ds(TOK // 2, TOK // 2))
    fwd = [
        remote(up_hbm.at[rows], dst.at[rows], fwd_send.at[i, k], fwd_recv.at[i, k], (to, after, tp))
        for i, rows in enumerate(parted)
        for k, (dst, to) in enumerate([(far, other), (near, rep)])
    ]
    for copy in fwd:
        copy.start()

    loads[5].wait()
    for first, sel, rank, count in ((0, sel_p, rank_p, kp), (SECTIONS, sel_f, rank_f, kf)):
        flags = [crosses[first + i] for i in range(SECTIONS)]
        seen = jnp.int32(0)
        chosen = [jnp.int32(0)] * count
        for i in range(SECTIONS):
            rank[i] = jnp.minimum(seen, count - 1)
            chosen = [
                jnp.where((flags[i] != 0) & (seen == k), i, chosen[k]) if k <= i else chosen[k]
                for k in range(count)
            ]
            seen = seen + flags[i]
        for k in range(count):
            sel[k] = chosen[k]

    for load in loads[:3]:
        load.wait()

    def grad_normed(j, _):
        cols = pl.ds(pl.multiple_of(j * WIDE, WIDE), WIDE)
        product = lax.dot_general(
            gv[...], w[cols, :], (((1,), (1,)), ((), ())), preferred_element_type=F32
        )
        gn[:, cols] = product * scale + go[:, cols].astype(F32)
        return _

    with jax.named_scope("grad_normed"):
        lax.fori_loop(0, W // WIDE, grad_normed, 0)
    parts[...] = jnp.zeros_like(parts)

    take_near = crosses[SECTIONS + before] == 0

    def statistics(j, rows):
        cols = lanes(j)
        x = jnp.where(take_near, near[rows, cols].astype(F32), far[rows, cols].astype(F32))
        near[rows, cols] = x.astype(BF16)
        parts[0, rows, :] += x * x
        parts[1, rows, :] += x * gain_ref[:, cols] * gn[rows, cols]

    for i, rows in enumerate(parted):
        with jax.named_scope("arrive"):
            for copy in fwd[2 * i : 2 * i + 2]:
                copy.wait_recv()
        with jax.named_scope("statistics"):
            each(0, BLOCKS, lambda j: statistics(j, rows))

    with jax.named_scope("statistics"):
        ones = jnp.full((8, LANE), 1.0, F32)
        row_id = lax.broadcasted_iota(jnp.int32, (8, LANE), 0)
        packed = jnp.zeros((8, LANE), F32)
        for i in range(2):
            row = lax.dot_general(
                ones, parts[i], (((1,), (1,)), ((), ())),
                preferred_element_type=F32, precision=lax.Precision.HIGHEST,
            )
            for k in range(3):
                packed = jnp.where(row_id == 3 * i + k, row[:, k * LANE : (k + 1) * LANE], packed)
        stat_send[...] = packed
        stat_recv[0] = packed
    for d in range(1, 8):
        remote(
            stat_send, stat_recv.at[d], stat_sem.at[0], stat_sem.at[1],
            (rep, sec, lax.rem(tp + d, 8)),
        ).start()
    stat_all = remote(
        stat_recv.at[pl.ds(1, 7)], stat_recv.at[pl.ds(1, 7)],
        stat_sem.at[0], stat_sem.at[1], (other, sec, tp),
    )
    with jax.named_scope("stat_wait"):
        stat_all.wait()

    def b_piece(j):
        return (pl.ds(pl.multiple_of(STRAIGHT + (j // 8) * HALF, 16), HALF), lanes(lax.rem(j, 8)))

    def b_scatter(d):
        q = column(d)
        return remote(
            grad.at[b_piece(q)], b_scat.at[sec], bs_sem.at[0], bs_sem.at[1], (rep, q, tp)
        )

    def b_gather(d):
        q = column(d)
        return remote(
            b_turn.at[q], ret_out.at[b_piece(sec)], bt_sem.at[0], bt_sem.at[1], (rep, q, tp)
        )

    def every(buffer, send_sem, recv_sem):
        ref = buffer.at[pl.ds(0, SECTIONS - 1)]
        return remote(ref, ref, send_sem, recv_sem, (other, sec, tp))

    b_scatter_all = every(b_scat, bs_sem.at[0], bs_sem.at[1])
    b_gather_all = every(b_turn, bt_sem.at[0], bt_sem.at[1])
    scatter_all = [every(scat[h], s_ss.at[h], s_rs.at[h]) for h in range(PHASES)]
    gather_all = [every(home.at[h], t_ss.at[h], t_rs.at[h]) for h in range(PHASES)]
    b_swap = remote(b_slot, b_cross, bx_sem.at[0], bx_sem.at[1], (other, sec, tp))

    def strip(h):
        return (h // 2, slice(None), pl.ds(WIDTH * (h % 2), WIDTH))

    def scatter(h, d):
        q = column(d)
        return remote(og.at[(q, *strip(h))], scat[h].at[sec], s_ss.at[h], s_rs.at[h], (rep, q, tp))

    def swap(h):
        return remote(slot.at[h], cross[h], x_ss.at[h], x_rs.at[h], (other, sec, tp))

    def gather(h, d):
        q = column(d)
        return remote(turn.at[h, q], home.at[h, sec], t_ss.at[h], t_rs.at[h], (rep, q, tp))

    with jax.named_scope("input_gradient"):
        total = jnp.sum(stat_recv[...], axis=0)
        for i in range(2):
            for k in range(3):
                spread = lax.dot_general(
                    total, jnp.where(row_id == 3 * i + k, 1.0, 0.0), (((0,), (0,)), ((), ())),
                    preferred_element_type=F32, precision=lax.Precision.HIGHEST,
                )
                parts[i, k * LANE : (k + 1) * LANE, :] = spread
        inv = lax.rsqrt(parts[0, 0:TOK, :] / D + eps)
        inv_ref[...] = inv
        dot_ref[...] = inv * inv * inv * parts[1, 0:TOK, :] / D

        def input_gradient(j, first, last):
            rows, cols = slice(first, last), lanes(j)
            x = near[rows, cols].astype(F32)
            grad[rows, cols] = (
                inv_ref[rows, :] * gain_ref[:, cols] * gn[rows, cols] - x * dot_ref[rows, :]
            ).astype(BF16)

        each(0, BLOCKS, lambda j: input_gradient(j, 0, STRAIGHT))
    first_rows = pl.ds(0, STRAIGHT)
    st_swap = remote(grad.at[first_rows], st_other, st_ss.at[0], st_rs.at[0], (other, sec, tp))
    st_hop = remote(st_out, ret_out.at[first_rows], st_ss.at[1], st_rs.at[1], (rep, before, tp))
    st_swap.start()

    def normalise(j):
        input_gradient(j, STRAIGHT, TOK)
        cols = lanes(j)
        x = near[:, cols].astype(F32)
        normed[:, cols] = (x * inv_ref[...] * gain_ref[:, cols]).astype(BF16)

    with jax.named_scope("normalise"):
        each(0, BLOCKS, normalise)
    each(1, SECTIONS, lambda d: b_scatter(d).start())
    mine = b_piece(sec)
    b_scat[sec] = grad[mine]

    with jax.named_scope("values"):
        out_row = lax.broadcasted_iota(jnp.int32, (PAD, TOK), 0)
        in_row = lax.broadcasted_iota(jnp.int32, (PAD, TOK), 1)
        place = lax.rem(out_row, ROWS)
        pick = jnp.where((in_row == (out_row // ROWS) * OWN + place) & (place < OWN), 1.0, 0.0)
        pick_ref[...] = pick.astype(BF16)

        def pad_rows(j):
            cols = pl.ds(pl.multiple_of(j * WIDE, WIDE), WIDE)
            padded[:, cols] = jnp.dot(
                pick_ref[...], normed[:, cols], preferred_element_type=F32
            ).astype(BF16)

        each(0, W // WIDE, pad_rows)

        def partial_values(j):
            cols = pl.ds(pl.multiple_of(j * WIDE, WIDE), WIDE)
            product = jnp.dot(padded[...], w[:, cols], preferred_element_type=F32) * scale
            vals[:, :, cols] = product.reshape(8, ROWS, WIDE)

        each(0, W // WIDE, partial_values)
        for z in range(4):
            vsend[z] = vals[2 * z + 1 - core].astype(BF16)
        core_copy = remote(vsend, vrecv, core_sem.at[0], core_sem.at[1], (rep, sec, sibling))
        core_copy.start()

    loads[3].wait()
    loads[4].wait()

    def outer_gradient(i):
        c = lax.rem(sec // 2 + i, BLOCKS)
        rows = lanes(c)
        weight_grad = lax.dot_general(
            normed[:, rows], gv[...], (((0,), (0,)), ((), ())), preferred_element_type=F32
        ) * scale
        local_new = w[rows, :].astype(F32) - inner_rate * weight_grad
        anchor = a[pl.ds(2 * c, 2)].reshape(LANE, W).astype(F32)
        og[pl.ds(2 * c, 2)] = (anchor - local_new).astype(BF16).reshape(2, STRIPS, 16, W)
        for e in range(2):
            d = lax.rem(2 * c + e - sec + SECTIONS, SECTIONS)

            @pl.when(d != 0)
            def _():
                scatter(0, d).start()

    with jax.named_scope("outer_gradient"):
        each(0, BLOCKS, outer_gradient)
    for h in range(PHASES):
        scat[h][sec] = og[(sec, *strip(h))]
    with jax.named_scope("values_send"):
        core_copy.wait()
        for d in range(1, 4):
            z = lax.rem(zlo + d, 4)
            zsend[d] = (vals[2 * z + core] + vrecv[z].astype(F32)).astype(BF16)
            remote(
                zsend.at[d], zrecv.at[d], z_sem.at[0], z_sem.at[1], (rep, sec, 2 * z + core)
            ).start()
    z_all = remote(
        zrecv.at[pl.ds(1, 3)], zrecv.at[pl.ds(1, 3)], z_sem.at[0], z_sem.at[1], (other, sec, tp)
    )
    each(1, SECTIONS, lambda d: scatter(1, d).start())

    def cross_back():
        with jax.named_scope("back_scatter_wait"):
            b_scatter_all.wait_recv()

        def fill(k):
            b_slot[k] = b_scat[lax.rem(sel_f[k] + 1, SECTIONS)]

        each(0, kf, fill)
        b_swap.start()

    def turn_back():
        def fill(i):
            flipped = crosses[SECTIONS + i] != 0
            crossed = b_cross[rank_f[i]].astype(F32)
            stayed = b_scat[lax.rem(i + 1, SECTIONS)].astype(F32)
            b_turn[i] = jnp.where(flipped, crossed, stayed).astype(BF16)

        each(0, SECTIONS, fill)
        each(1, SECTIONS, lambda d: b_gather(d).start())
        b_home.start()

    b_home = pltpu.make_async_copy(b_turn.at[sec], ret_out.at[mine], out_sem.at[2 * PHASES + 1])

    def cross_out(h):
        with jax.named_scope("scatter_wait"):
            scatter_all[h].wait_recv()

        def fill(k):
            slot[h, k] = scat[h][sel_p[k]]

        each(0, kp, fill)
        swap(h).start()

    def crossed_out(h):
        with jax.named_scope("cross_wait"):
            swap(h).wait_recv()

    def turn_out(h):
        def fill(i):
            turn[h, i] = cross[h][rank_p[i]]

        each(0, SECTIONS, fill)
        each(1, SECTIONS, lambda d: gather(h, d).start())
        home[h, sec] = turn[h, sec]

    paired = crosses[sec] != 0

    def out_copies(h):
        part = (slice(None), *strip(h))
        return (
            pltpu.make_async_copy(anc.at[part], anc_out.at[part], out_sem.at[h]),
            pltpu.make_async_copy(mom.at[part], mom_out.at[part], out_sem.at[h + PHASES]),
        )

    def outer_step(h):
        with jax.named_scope("gather_wait"):
            gather_all[h].wait_recv()

        def step(j):
            part = (j, *strip(h))
            own = og[part].astype(F32)
            chosen = jnp.where(paired, home[h, j].astype(F32), own)
            mean_grad = 0.5 * (own + chosen)
            momentum_next = keep_rate * m[part].astype(F32) + mean_grad
            anc[part] = (
                a[part].astype(F32) - outer_rate * (mean_grad + keep_rate * momentum_next)
            ).astype(BF16)
            mom[part] = momentum_next.astype(BF16)

        with jax.named_scope("outer_step"):
            each(0, SECTIONS, step)
        for copy in out_copies(h):
            copy.start()

    def send_out(h):
        if h < PHASES:
            each(1, SECTIONS, lambda d: scatter(h, d).start())

    def pass_on():
        with jax.named_scope("straight_wait"):
            st_swap.wait_recv()
        stays = crosses[SECTIONS + before] == 0

        def pick(j):
            cols = lanes(j)
            x = jnp.where(stays, grad[0:STRAIGHT, cols].astype(F32), st_other[:, cols].astype(F32))
            st_out[:, cols] = x.astype(BF16)

        each(0, BLOCKS, pick)
        st_hop.start()

    cross_back()
    send_out(2)
    cross_out(0)
    send_out(3)
    cross_out(1)
    send_out(4)
    send_out(5)
    pass_on()
    for h in range(2, 6):
        cross_out(h)
        send_out(h + 4)
    with jax.named_scope("back_cross_wait"):
        b_swap.wait_recv()
    turn_back()
    for h in range(PHASES):
        crossed_out(h)
        if h + 6 < PHASES:
            cross_out(h + 6)
        turn_out(h)
        send_out(h + 6+4)
        if h >= 2:
            outer_step(h - 2)

    total = vals[2 * zlo + core] + vrecv[zlo].astype(F32)
    with jax.named_scope("values_wait"):
        z_all.wait()
    for d in range(1, 4):
        total = total + zrecv[d].astype(F32)
    vout[...] = total.astype(BF16)
    val_copy = pltpu.make_async_copy(vout, val_out, out_sem.at[2 * PHASES])
    val_copy.start()


    outer_step(PHASES - 2)
    with jax.named_scope("back_gather_wait"):
        b_gather_all.wait_recv()
    outer_step(PHASES - 1)

    with jax.named_scope("finish"):
        for copy in fwd:
            copy.wait_send()
        b_swap.wait_send()
        for h in range(PHASES):
            swap(h).wait_send()

        for copy in [b_scatter_all, b_gather_all] + scatter_all + gather_all:
            copy.wait_send()
        b_home.wait()
        st_swap.wait_send()
        st_hop.wait()
        val_copy.wait()
        for h in range(PHASES):
            for copy in out_copies(h):
                copy.wait()


def finish_kernel(val, ret, anc, mom, val_out, ret_out, anc_out, mom_out, *scratch):
    into, out = scratch[-2:]
    parts = []
    for src, held, dst, cuts in zip(
        (anc, mom, ret), scratch[:3], (anc_out, mom_out, ret_out), (4, 4, 2)
    ):
        size = held.shape[0] // cuts
        for i in range(cuts):
            rows = pl.ds(i * size, size)
            n = len(parts)
            parts.append((
                pltpu.make_async_copy(src.at[rows], held.at[rows], into.at[n]),
                pltpu.make_async_copy(held.at[rows], dst.at[rows], out.at[n]),
            ))
    for first, _ in parts:
        first.start()
    val_out[...] = val[0:OWN, :]
    for first, second in parts:
        first.wait()
        second.start()
    for _, second in parts:
        second.wait()


def layer(kp, kf, collective_id, *args):
    any_spec = pl.BlockSpec(memory_space=pl.ANY)
    vmem_spec = pl.BlockSpec(memory_space=pltpu.VMEM)
    dma = pltpu.SemaphoreType.DMA
    tokens = pltpu.VMEM((TOK, W), BF16)
    square = pltpu.VMEM((W, W), BF16)
    cut = pltpu.VMEM((SECTIONS, STRIPS, 16, W), BF16)
    table = pltpu.SMEM((SECTIONS,), jnp.int32)

    def pieces(count):
        return pltpu.VMEM((count, HALF, LANE), BF16)

    def rows(count):
        return pltpu.VMEM((count, 16, WIDTH), BF16)

    def slots(count):
        return pltpu.VMEM((PHASES, count, 16, WIDTH), BF16)

    return pl.pallas_call(
        functools.partial(kernel, kp, kf),
        out_shape=(
            jax.ShapeDtypeStruct((ROWS, W), BF16),
            jax.ShapeDtypeStruct((TOK, W), BF16),
            jax.ShapeDtypeStruct((SECTIONS, STRIPS, 16, W), BF16),
            jax.ShapeDtypeStruct((SECTIONS, STRIPS, 16, W), BF16),
        ),
        in_specs=[any_spec, vmem_spec] + [any_spec] * 6,
        out_specs=(any_spec,) * 4,
        scratch_shapes=[
            tokens, tokens, tokens, tokens, square, cut, cut,
            pltpu.VMEM((TOK, W), F32),
            tokens,
            pltpu.VMEM((PAD, TOK), BF16),
            pltpu.VMEM((PAD, W), BF16),
            pltpu.VMEM((2, PAD, LANE), F32),
            pltpu.VMEM((8, LANE), F32),
            pltpu.VMEM((8, 8, LANE), F32),
            pltpu.VMEM((TOK, LANE), F32),
            pltpu.VMEM((TOK, LANE), F32),
            tokens,
            cut, cut, cut,
            pltpu.VMEM((8, ROWS, W), F32),
            pltpu.VMEM((4, ROWS, W), BF16),
            pltpu.VMEM((4, ROWS, W), BF16),
            pltpu.VMEM((4, ROWS, W), BF16),
            pltpu.VMEM((4, ROWS, W), BF16),
            pltpu.VMEM((ROWS, W), BF16),
            pieces(SECTIONS), pieces(kf), pieces(kf), pieces(SECTIONS),
            *[rows(SECTIONS)] * PHASES, slots(kp), *[rows(kp)] * PHASES, slots(SECTIONS), slots(SECTIONS),
            table, table, table, table, pltpu.SMEM((2 * SECTIONS,), jnp.int32),
            *[pltpu.VMEM((STRAIGHT, W), BF16)] * 2,
            dma((2,)), dma((2,)),
            dma((6,)), dma((2, 2)), dma((2, 2)), dma((2,)), dma((2,)), dma((2,)), dma((2 * PHASES + 2,)),
            dma((2,)), dma((2,)), dma((2,)),
            dma((PHASES,)), dma((PHASES,)), dma((PHASES,)), dma((PHASES,)), dma((PHASES,)), dma((PHASES,)),
        ],
        compiler_params=pltpu.CompilerParams(
            collective_id=collective_id, has_side_effects=True, vmem_limit_bytes=56 * 2**20
        ),
        cost_estimate=pl.CostEstimate(
            flops=6 * TOK * W * W, bytes_accessed=13 * 2**20, transcendentals=TOK * LANE
        ),
        name="layer",
    )(*args)


ROOM = ((6, 10), (8, 9), (8, 11), (9, 11), (11, 12), (SECTIONS, SECTIONS))


def room_kernel(pairing, routes, flags, branch):
    counts = []
    for first, table in ((0, pairing), (SECTIONS, routes)):
        count = jnp.int32(0)
        for i in range(SECTIONS):
            flag = table[0, i]
            flags[first + i] = flag
            count = count + flag
        counts.append(count)
    chosen = jnp.int32(len(ROOM) - 1)
    for i, (kp, kf) in reversed(list(enumerate(ROOM[:-1]))):
        chosen = jnp.where((counts[0] <= kp) & (counts[1] <= kf), i, chosen)
    branch[0] = chosen


def on_device(
    upstream, norm_gain, grad_values, grad_other, local_weights, anchor, momentum,
    section_routes, pairing,
):
    cut = (SECTIONS, STRIPS, 16, W)
    smem_spec = pl.BlockSpec(memory_space=pltpu.SMEM)
    flags, branch = pl.pallas_call(
        room_kernel,
        out_shape=(
            jax.ShapeDtypeStruct((2 * SECTIONS,), jnp.int32), jax.ShapeDtypeStruct((1,), jnp.int32)
        ),
        in_specs=[smem_spec] * 2,
        out_specs=(smem_spec,) * 2,
        name="room",
    )(pairing.T, section_routes.T)
    args = (
        upstream[0, 0], norm_gain[None, :], grad_values[0, 0], grad_other[0, 0],
        local_weights[0, 0], anchor.reshape(cut), momentum.reshape(cut), flags,
    )
    outs = lax.switch(
        branch[0], [functools.partial(layer, kp, kf, i) for i, (kp, kf) in enumerate(ROOM)], *args
    )
    any_spec = pl.BlockSpec(memory_space=pl.ANY)
    vmem_spec = pl.BlockSpec(memory_space=pltpu.VMEM)
    values, returned, anchor_new, momentum_new = pl.pallas_call(
        finish_kernel,
        out_shape=(
            jax.ShapeDtypeStruct((OWN, W), BF16),
            jax.ShapeDtypeStruct((TOK, W), BF16),
            jax.ShapeDtypeStruct(cut, BF16),
            jax.ShapeDtypeStruct(cut, BF16),
        ),
        in_specs=[vmem_spec] + [any_spec] * 3,
        out_specs=(vmem_spec,) + (any_spec,) * 3,
        scratch_shapes=[
            pltpu.VMEM(cut, BF16), pltpu.VMEM(cut, BF16), pltpu.VMEM((TOK, W), BF16),
            pltpu.SemaphoreType.DMA((10,)), pltpu.SemaphoreType.DMA((10,)),
        ],
        compiler_params=pltpu.CompilerParams(vmem_limit_bytes=32 * 2**20),
        name="finish",
    )(*outs)
    return (
        values[None, None],
        returned[None, None],
        anchor_new.reshape(1, 1, W, W),
        momentum_new.reshape(1, 1, W, W),
    )


def solution(mesh):
    return jax.shard_map(
        on_device,
        mesh=mesh,
        in_specs=(
            P("rep", "section", None, "tp"),
            P("tp"),
            P("rep", "section", None, None),
            P("rep", "section", None, "tp"),
            P("rep", "section", "tp", None),
            P("rep", "section", "tp", None),
            P("rep", "section", "tp", None),
            P(),
            P(),
        ),
        out_specs=(
            P("rep", "section", "tp", None),
            P("rep", "section", None, "tp"),
            P("rep", "section", "tp", None),
            P("rep", "section", "tp", None),
        ),
        check_vma=False,
    )
```
